256 devices in a mesh: dp: 64 (over z_lo, y, x), mp: 4 (over z_hi, core).
Axes of the slice: x: 4, y: 4, z: 8 (z_hi: 2, z_lo: 4; z = z_hi * 4 + z_lo), core: 2. Of those that a mesh axis runs over, the one named last changes fastest.
Arguments:
- tokens: bfloat16 [16384, 8192], P('dp', 'mp'), may hold values from -8 to 8
- attn_gain: bfloat16 [8192], replicated, may hold values from 0.5 to 1.5
- w_query: bfloat16 [8192, 4096], P('dp', 'mp'), may hold values from -2 to 2
- key_projection_weight: bfloat16 [8192, 512], P('dp', 'mp'), may hold values from -2 to 2
- value_projection_weight: bfloat16 [8192, 512], P('dp', 'mp'), may hold values from -0.0625 to 0.0625
- w_out: bfloat16 [4096, 8192], P('mp', 'dp'), may hold values from -0.09375 to 0.09375
- final_gain: bfloat16 [8192], P('mp'), may hold values from 0.5 to 1.5
- unembed: bfloat16 [64128, 8192], P('dp', 'mp'), may hold values from -0.29882812 to 0.29882812
- clean_ids: int32 [64], replicated, may hold values from 0 to 64127, as said below
- corrupt_ids: int32 [64], replicated, may hold values from 0 to 64127
Outputs:
- head_out: bfloat16 [16384, 4096], P('dp', 'mp')
- scores: float32 [64, 32], P('dp', 'mp')
- metric: float32 [64], P('dp')
The draws below stay inside these ranges and needn't reach their ends.
Inputs may be any that keep to these rules, and one draw needn't show every extreme that they name: `clean_ids`: split the ids into 64 aligned blocks of equal size and number the groups of 1 sequence alike; the block of a clean answer, minus the number of its sequence's group, taken modulo the number of blocks, is drawn so that every such offset occurs for some sequence.
All inputs are finite; a program needn't handle non-finite values.
Results may differ from the reference program's by a relative error of at most 0.015.
Values may be sent and summed in bfloat16 or wider, within the bound.
No kernel may reach another device: no remote copies, remote signals or barrier semaphores. Data moves between devices by JAX's collectives and lax.ppermute only.
A program may use at most 128 MiB of HBM per device.

```python
import math
import jax
import jax.numpy as jnp
from jax import lax

MODEL_WIDTH = 8192
QUERY_HEADS = 32
KEY_VALUE_HEADS = 4
HEAD_SIZE = 128
VOCAB = 64128
SEQUENCE_LENGTH = 256
SEQ_DEV = 1
SEQS = 64
TOKENS = 16384


def draw_tokens(key, part):
    key_common, key_jitter, key_shared = jax.random.split(jax.random.fold_in(key, 7), 3)
    common = jax.random.normal(key_common, (1, 1, MODEL_WIDTH), jnp.float32)
    ramp_up = jnp.arange(SEQS, dtype=jnp.float32) / max(SEQS - 1, 1)
    jitter = jax.random.uniform(key_jitter, (SEQS,), jnp.float32, 0.7, 1.3)
    perturbation_scale = 0.3 * 10.0 ** ramp_up * jitter
    random_perturbation = jax.random.normal(key_shared, (SEQS, SEQUENCE_LENGTH, MODEL_WIDTH), jnp.float32)
    drawn = random_perturbation + perturbation_scale[:, None, None] * common
    return jnp.clip(drawn, -8.0, 8.0).reshape(TOKENS, MODEL_WIDTH).astype(jnp.bfloat16)


def paired_weights(key):
    random_key_for_key = jax.random.fold_in(jax.random.fold_in(key, 23), 0)
    key_query = jax.random.fold_in(jax.random.fold_in(key, 23), 3)
    key_matrix = jax.random.normal(random_key_for_key, (MODEL_WIDTH, KEY_VALUE_HEADS * HEAD_SIZE), jnp.float32) / math.sqrt(MODEL_WIDTH)
    query_matrix = jax.random.normal(key_query, (MODEL_WIDTH, QUERY_HEADS * HEAD_SIZE), jnp.float32) / math.sqrt(MODEL_WIDTH)
    return (jnp.clip(query_matrix, -2.0, 2.0), jnp.clip(key_matrix, -2.0, 2.0))


def draw_w_query(key, part):
    return paired_weights(key)[0].astype(jnp.bfloat16)


def draw_key_projection_weight(key, part):
    return paired_weights(key)[1].astype(jnp.bfloat16)


def draw_clean_ids(key, part):
    key_order, key_inner = jax.random.split(jax.random.fold_in(key, 41), 2)
    group_count = SEQS // SEQ_DEV
    block_size = VOCAB // group_count
    shuffled = jax.random.permutation(key_order, group_count).astype(jnp.int32)
    offsets = (shuffled - shuffled[0] + group_count - 1) % group_count
    seq_index = jnp.arange(SEQS, dtype=jnp.int32)
    owner = seq_index // SEQ_DEV
    block = (owner + offsets[seq_index % group_count]) % group_count
    inner = jax.random.randint(key_inner, (SEQS,), 0, block_size, jnp.int32)
    inner = jnp.where(seq_index == 0, block_size - 1, inner)
    return (block * block_size + inner).astype(jnp.int32)


def set_ends(values, key, smallest, top_value):
    dims = values.shape
    spot = [jax.random.randint(jax.random.fold_in(key, axis), (), 0, dims[axis]) for axis in range(len(dims))]
    values = values.at[tuple(spot)].set(smallest)
    longest = dims.index(max(dims))
    spot[longest] = (spot[longest] + 1) % dims[longest]
    return values.at[tuple(spot)].set(top_value)


def level_of(rng, dims, shards, low, top_value):
    def one(axis_at, parts):
        heights = jax.random.uniform(jax.random.fold_in(jax.random.fold_in(rng, 6), axis_at), (parts,), jnp.float32, low / len(shards), top_value / len(shards))
        return jnp.repeat(jnp.exp(heights), dims[axis_at] // parts).reshape((-1,) + (1,) * (len(dims) - axis_at - 1))

    loudness = one(*shards[0])
    for cut in shards[1:]:
        loudness = loudness * one(*cut)
    return loudness


def normal_values(stream_key, extent, width, bound, pieces=(), kind=jnp.bfloat16):
    factor_of = level_of(stream_key, extent, pieces, -0.22, 0.18) if pieces else 1.0
    values = jax.random.normal(stream_key, extent, jnp.float32) * width * factor_of
    return jnp.minimum(jnp.maximum(values, -bound), bound).astype(kind)


def setup_inputs(seed: int = 0) -> dict:
    arg_keys = jax.random.split(jax.random.key(seed), 11)
    tokens = draw_tokens(jax.random.fold_in(arg_keys[10], 71), 0)
    attn_gain = jnp.clip(1.0 + 0.1 * jax.random.normal(arg_keys[1], (MODEL_WIDTH,), jnp.float32), 0.5, 1.5).astype(jnp.bfloat16)
    w_query = draw_w_query(jax.random.fold_in(arg_keys[10], 71), 0)
    key_projection_weight = draw_key_projection_weight(jax.random.fold_in(arg_keys[10], 71), 0)
    value_projection_weight = normal_values(arg_keys[4], (MODEL_WIDTH, KEY_VALUE_HEADS * HEAD_SIZE), MODEL_WIDTH ** -0.5, 0.0625, ((0, 64), (1, 4)))
    w_out = normal_values(arg_keys[5], (QUERY_HEADS * HEAD_SIZE, MODEL_WIDTH), (QUERY_HEADS * HEAD_SIZE) ** -0.5, 0.09375, ((0, 4), (1, 64)))
    final_gain = jnp.clip(1.0 + 0.1 * jax.random.normal(arg_keys[6], (MODEL_WIDTH,), jnp.float32), 0.5, 1.5).astype(jnp.bfloat16)
    unembed = normal_values(arg_keys[7], (VOCAB, MODEL_WIDTH), 0.05, 0.29882812, ((0, 64), (1, 4)))
    clean_ids = draw_clean_ids(jax.random.fold_in(arg_keys[10], 71), 0)
    corrupt_ids = set_ends(jax.random.randint(arg_keys[9], (SEQS,), 0, VOCAB), jax.random.fold_in(arg_keys[9], 1), 0, VOCAB - 1).astype(jnp.int32)
    return dict(tokens=tokens, attn_gain=attn_gain, w_query=w_query, key_projection_weight=key_projection_weight, value_projection_weight=value_projection_weight, w_out=w_out, final_gain=final_gain, unembed=unembed, clean_ids=clean_ids, corrupt_ids=corrupt_ids)


def apply_rotary(tensor, length):
    half_dim = tensor.shape[-1] // 2
    positions = jnp.arange(length, dtype=jnp.float32)
    inv_freq = jnp.exp(jnp.arange(half_dim, dtype=jnp.float32) * (-2.0 * math.log(500000.0) / tensor.shape[-1]))
    angles = positions[:, None] * inv_freq[None, :]
    cosine_table = jnp.cos(angles)[:, None, :]
    sine_table = jnp.sin(angles)[:, None, :]
    lower_half = tensor[..., :half_dim]
    upper_half = tensor[..., half_dim:]
    return jnp.concatenate([lower_half * cosine_table - upper_half * sine_table, upper_half * cosine_table + lower_half * sine_table], axis=-1)

def attend(queries, projected_key_rows, value_rows):
    length, q_heads, head_dim = queries.shape
    kv_heads = projected_key_rows.shape[1]
    grouped = queries.reshape(length, kv_heads, q_heads // kv_heads, head_dim)
    logits = jnp.einsum('tkgd,skd->kgts', grouped.astype(jnp.float32), projected_key_rows.astype(jnp.float32)) / math.sqrt(head_dim)
    causal = jnp.arange(length)[:, None] >= jnp.arange(length)[None, :]
    logits = jnp.where(causal, logits, -1e+30)
    row_top = lax.optimization_barrier(jnp.max(logits, axis=-1, keepdims=True))
    exponent = jnp.exp(logits - row_top)
    attn_probs = (exponent / lax.optimization_barrier(jnp.sum(exponent, axis=-1, keepdims=True))).astype(jnp.bfloat16)
    mixed_heads = jnp.einsum('kgts,skd->tkgd', attn_probs.astype(jnp.float32), value_rows.astype(jnp.float32))
    return mixed_heads.astype(jnp.bfloat16).reshape(length, q_heads * head_dim)

def reference(tokens, attn_gain, w_query, key_projection_weight, value_projection_weight, w_out, final_gain, unembed, clean_ids, corrupt_ids):

    def one_sequence(tokens_seq):
        wide = tokens_seq.astype(jnp.float32)
        normalized_rows = (wide * lax.rsqrt(lax.optimization_barrier(jnp.mean(wide * wide, axis=1, keepdims=True)) + 1e-05) * attn_gain.astype(jnp.float32)).astype(jnp.bfloat16)
        queries = apply_rotary(jnp.dot(normalized_rows, w_query, preferred_element_type=jnp.float32).reshape(SEQUENCE_LENGTH, QUERY_HEADS, HEAD_SIZE), SEQUENCE_LENGTH).astype(jnp.bfloat16)
        projected_key_rows = apply_rotary(jnp.dot(normalized_rows, key_projection_weight, preferred_element_type=jnp.float32).reshape(SEQUENCE_LENGTH, KEY_VALUE_HEADS, HEAD_SIZE), SEQUENCE_LENGTH).astype(jnp.bfloat16)
        value_rows = jnp.dot(normalized_rows, value_projection_weight, preferred_element_type=jnp.float32).astype(jnp.bfloat16).reshape(SEQUENCE_LENGTH, KEY_VALUE_HEADS, HEAD_SIZE)
        return attend(queries, projected_key_rows, value_rows)
    per_seq = lax.map(one_sequence, tokens.reshape(SEQS, SEQUENCE_LENGTH, MODEL_WIDTH))
    head_out = per_seq.reshape(TOKENS, QUERY_HEADS * HEAD_SIZE)
    head_mean = lax.optimization_barrier(jnp.sum(head_out.astype(jnp.float32), axis=0)) / TOKENS
    last_out = per_seq[:, SEQUENCE_LENGTH - 1, :]
    attn_last = jnp.dot(last_out, w_out, preferred_element_type=jnp.float32).astype(jnp.bfloat16)
    residual = tokens.reshape(SEQS, SEQUENCE_LENGTH, MODEL_WIDTH)[:, SEQUENCE_LENGTH - 1, :].astype(jnp.float32) + attn_last.astype(jnp.float32)
    direction = unembed[clean_ids].astype(jnp.float32) - unembed[corrupt_ids].astype(jnp.float32)
    weighted = final_gain.astype(jnp.float32) * direction
    inverse = lax.rsqrt(lax.optimization_barrier(jnp.mean(residual * residual, axis=1)) + 1e-05)
    metric = inverse * lax.optimization_barrier(jnp.sum(residual * weighted, axis=1))
    grad_last = (weighted * inverse[:, None] - residual * (metric * inverse * inverse / MODEL_WIDTH)[:, None]).astype(jnp.bfloat16)
    head_grads = jnp.dot(grad_last, w_out.T, preferred_element_type=jnp.float32)
    mean_gap = head_mean[None, :] - last_out.astype(jnp.float32)
    scores = lax.optimization_barrier(jnp.sum((mean_gap * head_grads).reshape(SEQS, QUERY_HEADS, HEAD_SIZE), axis=2))
    return (head_out, scores, metric)
```

```python
import math

import jax
import jax.numpy as jnp
from jax import lax
from jax.sharding import Mesh, PartitionSpec as P

MODEL_WIDTH = 8192
HEAD_SIZE = 128
LENGTH = 256
TOKENS = 16384
DP = ("zl", "y", "x")
MP = ("zh", "c")
F32 = jnp.float32
BF16 = jnp.bfloat16


def from_everyone(value, axis):
    count = lax.axis_size(axis)
    return lax.all_to_all(
        jnp.broadcast_to(value[None], (count, *value.shape)), axis, 0, 0, tiled=True
    )


def send(value, route):
    pairs = []
    for x in range(4):
        for c in range(2):
            to = route(x, c)
            if to is not None:
                pairs.append((x * 2 + c, (to[0] % 4) * 2 + to[1]))
    return lax.ppermute(value, ("x", "c"), pairs)


def rotary_tables():
    half = HEAD_SIZE // 2
    positions = jnp.arange(LENGTH, dtype=F32)
    inv_freq = jnp.exp(
        jnp.arange(half, dtype=F32) * (-2.0 * math.log(500000.0) / HEAD_SIZE)
    )
    angles = positions[:, None] * inv_freq[None, :]
    return jnp.cos(angles)[:, None, :], jnp.sin(angles)[:, None, :]


def rotate(t, cos, sin):
    half = HEAD_SIZE // 2
    lo, hi = t[..., :half], t[..., half:]
    return jnp.concatenate([lo * cos - hi * sin, hi * cos + lo * sin], axis=-1)


def ring_share(block, core):
    pa = send(block, lambda x, c: (x - 1, 0) if c == 0 else (x + 1, 1))
    pb = send(block, lambda x, c: (x + 1, 1) if c == 0 else (x - 1, 0))
    pc = send(block, lambda x, c: (x + 2, 1) if c == 0 else (x, 0))
    pd = send(block, lambda x, c: None if c == 0 else (x + 2, 1))
    first = core == 0
    f0 = jnp.concatenate([jnp.where(first, block, pc), jnp.where(first, pa, pb)], axis=0)
    f1 = jnp.concatenate([jnp.where(first, pc, pd), jnp.where(first, pb, pa)], axis=0)
    return f0, f1


def per_device(tokens, gain, w_query, w_key, w_value, w_out, final_gain, unembed, clean, corrupt):
    zh, core, x = lax.axis_index("zh"), lax.axis_index("c"), lax.axis_index("x")
    odd = x % 2

    with jax.named_scope("weights"):
        wkv = jnp.concatenate([w_key, w_value], axis=1)
        width = w_query.shape[1] // 2
        mine = lax.dynamic_slice_in_dim(w_query, odd * width, width, 1)
        other = lax.dynamic_slice_in_dim(w_query, (1 - odd) * width, width, 1)
        pa = send(jnp.concatenate([mine, wkv], axis=1), lambda x, c: (2 * c + x % 2, x // 2))
        pb = send(jnp.concatenate([other, wkv], axis=1), lambda x, c: (2 * c + 1 - x % 2, x // 2))
        rows = jnp.concatenate(
            [jnp.where(odd == 0, pa, pb), jnp.where(odd == 0, pb, pa)], axis=0
        )
        along_z = lax.all_gather(rows, "zl", axis=0)
        order = [2 * zh, 2 * zh + 1, 2 - 2 * zh, 3 - 2 * zh]
        weights = [
            lax.all_gather(
                lax.dynamic_index_in_dim(along_z, m, 0, keepdims=False),
                ("y", "c"),
                axis=0,
                tiled=True,
            )
            for m in order
        ]

    with jax.named_scope("tokens"):
        far = lax.ppermute(tokens, "zh", [(0, 1), (1, 0)])
        chunks = ring_share(tokens, core) + ring_share(far, core)

    with jax.named_scope("direction"):
        vocab_rows = unembed.shape[0]
        dp_index = lax.axis_index(DP)
        ids = dp_index * vocab_rows + jnp.arange(vocab_rows, dtype=jnp.int32)
        one_hot = (clean[:, None] == ids[None, :]).astype(F32) - (
            corrupt[:, None] == ids[None, :]
        ).astype(F32)
        found = jnp.dot(one_hot.astype(BF16), unembed, preferred_element_type=F32)
        direction = jnp.sum(lax.all_to_all(found[:, None], DP, 0, 0, tiled=True), axis=0)
        weighted = final_gain.astype(F32) * direction[0]
        both = jnp.stack([weighted, tokens[LENGTH - 1].astype(F32)])
        wide = jnp.moveaxis(from_everyone(both, MP), 0, 1).reshape(2, 64, 128)
        columns = lax.all_to_all(jnp.moveaxis(wide, 1, 0), DP, 0, 0, tiled=True)
        weighted_cols, token_cols = columns[:, 0], columns[:, 1]
        back_w = lax.dot_general(
            weighted_cols.astype(BF16), w_out, (((1,), (1,)), ((), ())), preferred_element_type=F32
        )
        grad_w = jnp.sum(lax.all_to_all(back_w[:, None], DP, 0, 0, tiled=True), axis=0)[0]

    with jax.named_scope("project"):
        acc, squares = 0.0, 0.0
        for m, chunk, weight in zip(order, chunks, weights):
            t = chunk.astype(F32)
            g = lax.dynamic_slice_in_dim(gain, m * t.shape[1], t.shape[1], 0).astype(F32)
            squares = squares + jnp.sum(t * t, axis=1, keepdims=True)
            acc = acc + jnp.dot((t * g).astype(BF16), weight, preferred_element_type=F32)
        acc = acc * lax.rsqrt(squares / MODEL_WIDTH + 1e-05)
        heads = width // HEAD_SIZE
        acc = acc.reshape(2, LENGTH, heads + 2, HEAD_SIZE)
        cos, sin = rotary_tables()
        queries = rotate(acc[:, :, :heads], cos, sin).astype(BF16)
        keys = rotate(acc[:, :, heads : heads + 1], cos, sin)[:, :, 0].astype(BF16)
        values = acc[:, :, heads + 1].astype(BF16)

    with jax.named_scope("attend"):
        logits = jnp.einsum("btgd,bsd->bgts", queries, keys, preferred_element_type=F32)
        logits = logits / math.sqrt(HEAD_SIZE)
        causal = jnp.arange(LENGTH)[:, None] >= jnp.arange(LENGTH)[None, :]
        logits = jnp.where(causal, logits, -1e30)
        top = jnp.max(logits, axis=-1, keepdims=True)
        e = jnp.exp(logits - top)
        probs = (e / jnp.sum(e, axis=-1, keepdims=True)).astype(BF16)
        mixed = jnp.einsum("bgts,bsd->btgd", probs, values, preferred_element_type=F32)
        mixed = mixed.astype(BF16).reshape(2, LENGTH, width)

    with jax.named_scope("return_heads"):
        oa = send(mixed[0], lambda x, c: (x, x // 2) if c == 0 else (x + 2, x // 2))
        ob = send(mixed[1], lambda x, c: (x + 1, x // 2) if c == 0 else (x - 1, x // 2))
        head_out = jnp.concatenate(
            [jnp.where(odd == 0, oa, ob), jnp.where(odd == 0, ob, oa)], axis=1
        )

    with jax.named_scope("tail"):
        last = head_out[LENGTH - 1].astype(F32)
        total = jnp.sum(head_out.astype(F32), axis=0)
        every = from_everyone(jnp.stack([last, total]), DP)
        head_mean = jnp.sum(every[:, 1], axis=0) / TOKENS
        part = jnp.dot(every[:, 0].astype(BF16), w_out, preferred_element_type=F32)
        attn_last = jnp.sum(from_everyone(part, MP), axis=0).astype(BF16)
        residual = token_cols + attn_last.astype(F32)
        back_r = lax.dot_general(
            residual.astype(BF16), w_out, (((1,), (1,)), ((), ())), preferred_element_type=F32
        )
        sums = jnp.concatenate(
            [
                jnp.broadcast_to(jnp.sum(residual * residual, axis=1)[:, None], (64, 64)),
                jnp.broadcast_to(jnp.sum(residual * weighted_cols, axis=1)[:, None], (64, 64)),
            ],
            axis=1,
        )
        packed = jnp.concatenate([back_r, sums], axis=1)
        mine = jnp.sum(lax.all_to_all(packed[:, None], DP, 0, 0, tiled=True), axis=0)[0]
        grad_r, square, product = mine[:1024], mine[1024], mine[1024 + 64]
        inverse = lax.rsqrt(square / MODEL_WIDTH + 1e-05)
        metric = inverse * product
        head_grads = grad_w * inverse - grad_r * (metric * inverse * inverse / MODEL_WIDTH)
        scores = jnp.sum(((head_mean - last) * head_grads).reshape(1, 8, HEAD_SIZE), axis=2)
    return head_out, scores, metric[None]


def solution(mesh):
    fine = Mesh(mesh.devices.reshape(4, 4, 4, 2, 2), (*DP, *MP))
    in_specs = (
        P(DP, MP),
        P(),
        P(DP, MP),
        P(DP, MP),
        P(DP, MP),
        P(MP, DP),
        P(MP),
        P(DP, MP),
        P(),
        P(),
    )
    out_specs = (P(DP, MP), P(DP, MP), P(DP))
    return jax.shard_map(
        per_device, mesh=fine, in_specs=in_specs, out_specs=out_specs, check_vma=False
    )
```

```python
import math

import jax
import jax.numpy as jnp
from jax import lax
from jax.sharding import Mesh, PartitionSpec as P

MODEL_WIDTH = 8192
HEAD_SIZE = 128
LENGTH = 256
TOKENS = 16384
DP = ("zl", "y", "x")
MP = ("zh", "c")
F32 = jnp.float32
BF16 = jnp.bfloat16


def from_everyone(value, axis):
    count = lax.axis_size(axis)
    return lax.all_to_all(
        jnp.broadcast_to(value[None], (count, *value.shape)), axis, 0, 0, tiled=True
    )


def send(value, route):
    pairs = []
    for x in range(4):
        for c in range(2):
            to = route(x, c)
            if to is not None:
                pairs.append((x * 2 + c, (to[0] % 4) * 2 + to[1]))
    return lax.ppermute(value, ("x", "c"), pairs)


def rotary_tables():
    half = HEAD_SIZE // 2
    positions = jnp.arange(LENGTH, dtype=F32)
    inv_freq = jnp.exp(
        jnp.arange(half, dtype=F32) * (-2.0 * math.log(500000.0) / HEAD_SIZE)
    )
    angles = positions[:, None] * inv_freq[None, :]
    return jnp.cos(angles)[:, None, :], jnp.sin(angles)[:, None, :]


def rotate(t, cos, sin):
    half = HEAD_SIZE // 2
    lo, hi = t[..., :half], t[..., half:]
    return jnp.concatenate([lo * cos - hi * sin, hi * cos + lo * sin], axis=-1)


def ring_share(block, core):
    first = core == 0
    pa = send(block, lambda x, c: (x - 1, 0) if c == 0 else (x + 1, 1))
    pb = send(block, lambda x, c: (x + 1, 1) if c == 0 else (x - 1, 0))
    pc = send(jnp.where(first, pa, block), lambda x, c: (x - 1, 1) if c == 0 else (x, 0))
    pd = send(pa, lambda x, c: None if c == 0 else (x + 1, 1))
    f0 = jnp.concatenate([jnp.where(first, block, pc), jnp.where(first, pa, pb)], axis=0)
    f1 = jnp.concatenate([jnp.where(first, pc, pd), jnp.where(first, pb, pa)], axis=0)
    return f0, f1


def per_device(tokens, gain, w_query, w_key, w_value, w_out, final_gain, unembed, clean, corrupt):
    zh, core, x = lax.axis_index("zh"), lax.axis_index("c"), lax.axis_index("x")
    odd = x % 2

    with jax.named_scope("weights"):
        wkv = jnp.concatenate([w_key, w_value], axis=1)
        width = w_query.shape[1] // 2
        mine = lax.dynamic_slice_in_dim(w_query, odd * width, width, 1)
        other = lax.dynamic_slice_in_dim(w_query, (1 - odd) * width, width, 1)
        pa = send(jnp.concatenate([mine, wkv], axis=1), lambda x, c: (2 * c + x % 2, x // 2))
        pb = send(jnp.concatenate([other, wkv], axis=1), lambda x, c: (2 * c + 1 - x % 2, x // 2))
        rows = jnp.concatenate(
            [jnp.where(odd == 0, pa, pb), jnp.where(odd == 0, pb, pa)], axis=0
        )
        weights = lax.all_gather(rows, ("zl", "y", "c"), axis=0, tiled=True)

    with jax.named_scope("tokens"):
        far = lax.ppermute(tokens, "zh", [(0, 1), (1, 0)])
        chunks = ring_share(tokens, core) + ring_share(far, core)

    with jax.named_scope("direction"):
        vocab_rows = unembed.shape[0]
        dp_index = lax.axis_index(DP)
        ids = dp_index * vocab_rows + jnp.arange(vocab_rows, dtype=jnp.int32)
        one_hot = (clean[:, None] == ids[None, :]).astype(F32) - (
            corrupt[:, None] == ids[None, :]
        ).astype(F32)
        found = jnp.dot(one_hot.astype(BF16), unembed, preferred_element_type=F32)
        direction = jnp.sum(lax.all_to_all(found[:, None], DP, 0, 0, tiled=True), axis=0)
        weighted = final_gain.astype(F32) * direction[0]
        both = jnp.stack([weighted, tokens[LENGTH - 1].astype(F32)])
        wide = jnp.moveaxis(from_everyone(both, MP), 0, 1).reshape(2, 64, 128)
        columns = lax.all_to_all(jnp.moveaxis(wide, 1, 0), DP, 0, 0, tiled=True)
        weighted_cols, token_cols = columns[:, 0], columns[:, 1]
        back_w = lax.dot_general(
            weighted_cols.astype(BF16), w_out, (((1,), (1,)), ((), ())), preferred_element_type=F32
        )
        grad_w = jnp.sum(lax.all_to_all(back_w[:, None], DP, 0, 0, tiled=True), axis=0)[0]

    with jax.named_scope("scale"):
        order = [2 * zh, 2 * zh + 1, 2 - 2 * zh, 3 - 2 * zh]
        scaled, squares = [], 0.0
        for m, chunk in zip(order, chunks):
            t = chunk.astype(F32)
            g = lax.dynamic_slice_in_dim(gain, m * t.shape[1], t.shape[1], 0).astype(F32)
            squares = squares + jnp.sum(t * t, axis=1, keepdims=True)
            scaled.append((t * g).astype(BF16))
        *scaled, squares, weights, weighted_cols, token_cols, grad_w = lax.optimization_barrier(
            (*scaled, squares, weights, weighted_cols, token_cols, grad_w)
        )

    with jax.named_scope("project"):
        acc, depth = 0.0, scaled[0].shape[1]
        for m, t in zip(order, scaled):
            weight = lax.dynamic_slice_in_dim(weights, m * depth, depth, 0)
            acc = acc + jnp.dot(t, weight, preferred_element_type=F32)
        acc = acc * lax.rsqrt(squares / MODEL_WIDTH + 1e-05)
        heads = width // HEAD_SIZE
        acc = acc.reshape(2, LENGTH, heads + 2, HEAD_SIZE)
        cos, sin = rotary_tables()
        queries = rotate(acc[:, :, :heads], cos, sin).astype(BF16)
        keys = rotate(acc[:, :, heads : heads + 1], cos, sin)[:, :, 0].astype(BF16)
        values = acc[:, :, heads + 1].astype(BF16)

    with jax.named_scope("attend"):
        logits = jnp.einsum("btgd,bsd->bgts", queries, keys, preferred_element_type=F32)
        logits = logits / math.sqrt(HEAD_SIZE)
        causal = jnp.arange(LENGTH)[:, None] >= jnp.arange(LENGTH)[None, :]
        logits = jnp.where(causal, logits, -1e30)
        top = jnp.max(logits, axis=-1, keepdims=True)
        e = jnp.exp(logits - top)
        probs = (e / jnp.sum(e, axis=-1, keepdims=True)).astype(BF16)
        mixed = jnp.einsum("bgts,bsd->btgd", probs, values, preferred_element_type=F32)
        mixed = mixed.astype(BF16).reshape(2, LENGTH, width)

    with jax.named_scope("return_heads"):
        oa = send(mixed[0], lambda x, c: (x, x // 2) if c == 0 else (x + 2, x // 2))
        ob = send(mixed[1], lambda x, c: (x + 1, x // 2) if c == 0 else (x - 1, x // 2))
        head_out = jnp.concatenate(
            [jnp.where(odd == 0, oa, ob), jnp.where(odd == 0, ob, oa)], axis=1
        )

    with jax.named_scope("tail"):
        last = head_out[LENGTH - 1].astype(F32)
        total = jnp.sum(head_out.astype(F32), axis=0)
        every = from_everyone(jnp.stack([last, total]), DP)
        head_mean = jnp.sum(every[:, 1], axis=0) / TOKENS
        part = jnp.dot(every[:, 0].astype(BF16), w_out, preferred_element_type=F32)
        attn_last = jnp.sum(from_everyone(part, MP), axis=0).astype(BF16)
        residual = token_cols + attn_last.astype(F32)
        back_r = lax.dot_general(
            residual.astype(BF16), w_out, (((1,), (1,)), ((), ())), preferred_element_type=F32
        )
        sums = jnp.concatenate(
            [
                jnp.broadcast_to(jnp.sum(residual * residual, axis=1)[:, None], (64, 64)),
                jnp.broadcast_to(jnp.sum(residual * weighted_cols, axis=1)[:, None], (64, 64)),
            ],
            axis=1,
        )
        packed = jnp.concatenate([back_r, sums], axis=1)
        mine = jnp.sum(lax.all_to_all(packed[:, None], DP, 0, 0, tiled=True), axis=0)[0]
        grad_r, square, product = mine[:1024], mine[1024], mine[1024 + 64]
        inverse = lax.rsqrt(square / MODEL_WIDTH + 1e-05)
        metric = inverse * product
        head_grads = grad_w * inverse - grad_r * (metric * inverse * inverse / MODEL_WIDTH)
        scores = jnp.sum(((head_mean - last) * head_grads).reshape(1, 8, HEAD_SIZE), axis=2)
    return head_out, scores, metric[None]


def solution(mesh):
    fine = Mesh(mesh.devices.reshape(4, 4, 4, 2, 2), (*DP, *MP))
    in_specs = (
        P(DP, MP),
        P(),
        P(DP, MP),
        P(DP, MP),
        P(DP, MP),
        P(MP, DP),
        P(MP),
        P(DP, MP),
        P(),
        P(),
    )
    out_specs = (P(DP, MP), P(DP, MP), P(DP))
    return jax.shard_map(
        per_device, mesh=fine, in_specs=in_specs, out_specs=out_specs, check_vma=False
    )
```

```python
import math

import jax
import jax.numpy as jnp
from jax import lax
from jax.sharding import Mesh, PartitionSpec as P

MODEL_WIDTH = 8192
HEAD_SIZE = 128
LENGTH = 256
TOKENS = 16384
DP = ("zl", "y", "x")
MP = ("zh", "c")
F32 = jnp.float32
BF16 = jnp.bfloat16


def from_everyone(value, axis):
    count = lax.axis_size(axis)
    return lax.all_to_all(
        jnp.broadcast_to(value[None], (count, *value.shape)), axis, 0, 0, tiled=True
    )


def send(value, route):
    pairs = []
    for z in range(4):
        for c in range(2):
            to = route(z, c)
            pairs.append((z * 2 + c, (to[0] % 4) * 2 + to[1]))
    return lax.ppermute(value, ("zl", "c"), pairs)


def along(value, step):
    place = lambda z: (z % 4) * 2 + z // 4
    pairs = [(place(z), place((z + step) % 8)) for z in range(8)]
    return lax.ppermute(value, ("zl", "zh"), pairs)


def swap_cores(value):
    return lax.ppermute(value, "c", [(0, 1), (1, 0)])


def rotary_tables():
    half = HEAD_SIZE // 2
    positions = jnp.arange(LENGTH, dtype=F32)
    inv_freq = jnp.exp(
        jnp.arange(half, dtype=F32) * (-2.0 * math.log(500000.0) / HEAD_SIZE)
    )
    angles = positions[:, None] * inv_freq[None, :]
    return jnp.cos(angles)[:, None, :], jnp.sin(angles)[:, None, :]


def rotate(t, cos, sin):
    half = HEAD_SIZE // 2
    lo, hi = t[..., :half], t[..., half:]
    return jnp.concatenate([lo * cos - hi * sin, hi * cos + lo * sin], axis=-1)


def ring_share(block):
    cut = block.shape[0] // 2
    own = (block[:cut], block[cut:])
    got = {0: own}
    for sign in (1, -1):
        now = own
        for r in (1, 2, 3):
            now = tuple(along(v, sign) for v in now)
            got[-sign * r] = now
    got[4] = (along(got[-3][0], 1), along(got[3][1], -1))
    return got


def per_device(tokens, gain, w_query, w_key, w_value, w_out, final_gain, unembed, clean, corrupt):
    zh, zl, core = lax.axis_index("zh"), lax.axis_index("zl"), lax.axis_index("c")
    yx = lax.axis_index(("y", "x"))
    first = core == 0
    even = zl % 2 == 0
    width = w_query.shape[1] // 2

    with jax.named_scope("weights"):
        wkv = jnp.concatenate([w_key, w_value], axis=1)
        upper = zl // 2
        pieces = [
            jnp.concatenate(
                [lax.dynamic_slice_in_dim(w_query, h * width, width, 1), wkv], axis=1
            )
            for h in (upper, 1 - upper)
        ]
        pa = send(pieces[0], lambda z, c: (2 * c + z // 2, z % 2))
        pb = send(pieces[1], lambda z, c: (2 * c + 1 - z // 2, z % 2))
        rows = jnp.concatenate([jnp.where(even, pa, pb), jnp.where(even, pb, pa)], axis=1)
        weights = lax.all_gather(rows, ("y", "x"), axis=0, tiled=True)

    with jax.named_scope("tokens"):
        blocks = ring_share(tokens)

    with jax.named_scope("direction"):
        vocab_rows = unembed.shape[0]
        ids = lax.axis_index(DP) * vocab_rows + jnp.arange(vocab_rows, dtype=jnp.int32)
        one_hot = (clean[:, None] == ids[None, :]).astype(F32) - (
            corrupt[:, None] == ids[None, :]
        ).astype(F32)
        found = jnp.dot(one_hot.astype(BF16), unembed, preferred_element_type=F32)
        found = found.reshape(4, 16, 16, 128).swapaxes(1, 2).astype(BF16)
        here = (jnp.arange(4) == zl)[:, None, None, None]
        own_last = jnp.where(here, tokens[LENGTH - 1].reshape(1, 16, 1, 128), 0).astype(BF16)
        packed = jnp.concatenate([found, own_last], axis=2).reshape(64, 17, 128)
        packed, _ = lax.optimization_barrier((packed, blocks[1][0]))
        packed = lax.all_to_all(packed, DP, 0, 0, tiled=True).astype(F32)
        packed = jnp.sum(packed.reshape(4, 16, 17, 128), axis=0)
        gain_cols = lax.dynamic_slice_in_dim(final_gain, yx * 128, 128, 0).astype(F32)
        weighted = gain_cols * jnp.sum(packed[:, :16], axis=0)
        both = jnp.stack([weighted, packed[:, 16]])
        both, _ = lax.optimization_barrier((both, blocks[2][0]))
        both = from_everyone(both, ("zl", "zh", "c")).reshape(4, 4, 2, 16, 128)
        both = lax.dynamic_index_in_dim(both, zl, 1, keepdims=False)
        weighted_cols = both[:, 0].reshape(64, 128)
        token_cols = both[:, 1].reshape(64, 128)
        back_w = lax.dot_general(
            weighted_cols.astype(BF16), w_out, (((1,), (1,)), ((), ())), preferred_element_type=F32
        )
        back_w, _ = lax.optimization_barrier((back_w, blocks[3][0]))
        grad_w = jnp.sum(lax.all_to_all(back_w[:, None], DP, 0, 0, tiled=True), axis=0)[0]
        other = swap_cores(w_out)
        w_half = jnp.concatenate(
            [jnp.where(first, w_out, other), jnp.where(first, other, w_out)], axis=0
        )

    with jax.named_scope("scale"):
        scaled, squares, sides = {}, {}, {}
        depth = tokens.shape[1]
        for k, parts in blocks.items():
            side = ((zh * 4 + zl + k) % 8) // 4
            g = lax.dynamic_slice_in_dim(gain, (2 * side + core) * depth, depth, 0).astype(F32)
            t = jnp.concatenate(parts, axis=0).astype(F32)
            squares[k] = jnp.sum(t * t, axis=1, keepdims=True)
            scaled[k] = (t * g).astype(BF16)
            sides[k] = side
        scaled, squares = lax.optimization_barrier((scaled, squares))

    with jax.named_scope("project"):
        columns = width + 2 * HEAD_SIZE

        def project(k):
            weight = lax.dynamic_slice_in_dim(weights, sides[k] * columns, columns, 1)
            return jnp.dot(scaled[k], weight, preferred_element_type=F32)

        sums = []
        for near, far in ((0, 4), (1, -3), (2, -2), (-1, 3)):
            sums.append((project(near) + project(far), squares[near] + squares[far]))

        def across(low, high):
            kept = [jnp.where(first, a, b) for a, b in zip(low, high)]
            sent = [jnp.where(first, b, a) for a, b in zip(low, high)]
            total, square = [a + swap_cores(b) for a, b in zip(kept, sent)]
            return total * lax.rsqrt(square / MODEL_WIDTH + 1e-05)

        late = across(sums[1], sums[3])
        acc = jnp.stack([across(sums[0], sums[2]), late])
        acc, grad_w, w_half = lax.optimization_barrier((acc, grad_w, w_half))
        heads = width // HEAD_SIZE
        acc = acc.reshape(2, LENGTH, heads + 2, HEAD_SIZE)
        cos, sin = rotary_tables()
        queries = rotate(acc[:, :, :heads], cos, sin).astype(BF16)
        keys = rotate(acc[:, :, heads : heads + 1], cos, sin)[:, :, 0].astype(BF16)
        values = acc[:, :, heads + 1].astype(BF16)

    with jax.named_scope("attend"):
        logits = jnp.einsum("btgd,bsd->bgts", queries, keys, preferred_element_type=F32)
        logits = logits / math.sqrt(HEAD_SIZE)
        causal = jnp.arange(LENGTH)[:, None] >= jnp.arange(LENGTH)[None, :]
        logits = jnp.where(causal, logits, -1e30)
        top = jnp.max(logits, axis=-1, keepdims=True)
        e = jnp.exp(logits - top)
        probs = (e / jnp.sum(e, axis=-1, keepdims=True)).astype(BF16)
        mixed = jnp.einsum("bgts,bsd->btgd", probs, values, preferred_element_type=F32)
        mixed = mixed.astype(BF16).reshape(2, LENGTH, width)

    with jax.named_scope("return_heads"):
        oa = send(mixed[0], lambda z, c: (z, z // 2) if c == 0 else (z + 2, z // 2))
        ob = send(mixed[1], lambda z, c: (z + 1, z // 2) if c == 0 else (z - 1, z // 2))
        head_out = jnp.concatenate(
            [jnp.where(even, oa, ob), jnp.where(even, ob, oa)], axis=1
        )

    with jax.named_scope("tail"):
        every = from_everyone(mixed[:, LENGTH - 1], DP).reshape(4, 16, 2, width)
        part = jnp.einsum(
            "xpsd,xdn->sxpn", every, w_half.reshape(4, width, 128), preferred_element_type=F32
        )
        part = jnp.where(
            first,
            part[0] + jnp.roll(part[1], 1, axis=0),
            jnp.roll(part[0], 2, axis=0) + jnp.roll(part[1], -1, axis=0),
        ).reshape(64, 128)
        attn_last = jnp.sum(from_everyone(part, MP), axis=0).astype(BF16)
        residual = token_cols + attn_last.astype(F32)
        back_r = lax.dot_general(
            residual.astype(BF16), w_out, (((1,), (1,)), ((), ())), preferred_element_type=F32
        )
        extra = jnp.concatenate(
            [
                jnp.broadcast_to(jnp.sum(residual * residual, axis=1)[:, None], (64, 64)),
                jnp.broadcast_to(jnp.sum(residual * weighted_cols, axis=1)[:, None], (64, 64)),
            ],
            axis=1,
        )
        packed = jnp.concatenate([back_r, extra], axis=1)
        mine = jnp.sum(lax.all_to_all(packed[:, None], DP, 0, 0, tiled=True), axis=0)[0]
        grad_r, square, product = mine[:1024], mine[1024], mine[1024 + 64]
        inverse = lax.rsqrt(square / MODEL_WIDTH + 1e-05)
        metric = inverse * product
        head_grads = grad_w * inverse - grad_r * (metric * inverse * inverse / MODEL_WIDTH)
        total = jnp.sum(head_out.astype(F32), axis=0)
        head_mean = jnp.sum(from_everyone(total[None], DP), axis=(0, 1)) / TOKENS
        last = head_out[LENGTH - 1].astype(F32)
        scores = jnp.sum(((head_mean - last) * head_grads).reshape(1, 8, HEAD_SIZE), axis=2)
    return head_out, scores, metric[None]


def solution(mesh):
    fine = Mesh(mesh.devices.reshape(4, 4, 4, 2, 2), (*DP, *MP))
    in_specs = (
        P(DP, MP),
        P(),
        P(DP, MP),
        P(DP, MP),
        P(DP, MP),
        P(MP, DP),
        P(MP),
        P(DP, MP),
        P(),
        P(),
    )
    out_specs = (P(DP, MP), P(DP, MP), P(DP))
    return jax.shard_map(
        per_device, mesh=fine, in_specs=in_specs, out_specs=out_specs, check_vma=False
    )
```

```python
import functools
import math

import jax
import jax.numpy as jnp
from jax import lax
from jax.experimental import pallas as pl
from jax.experimental.pallas import tpu as pltpu
from jax.sharding import Mesh, PartitionSpec as P

MODEL_WIDTH = 8192
HEAD_SIZE = 128
LENGTH = 256
TOKENS = 16384
DP = ("zl", "y", "x")
MP = ("zh", "c")
F32 = jnp.float32
BF16 = jnp.bfloat16


def from_everyone(value, axis):
    count = lax.axis_size(axis)
    return lax.all_to_all(
        jnp.broadcast_to(value[None], (count, *value.shape)), axis, 0, 0, tiled=True
    )


def send(value, route):
    pairs = []
    for z in range(4):
        for c in range(2):
            to = route(z, c)
            pairs.append((z * 2 + c, (to[0] % 4) * 2 + to[1]))
    return lax.ppermute(value, ("zl", "c"), pairs)


def along(value, step):
    place = lambda z: (z % 4) * 2 + z // 4
    pairs = [(place(z), place((z + step) % 8)) for z in range(8)]
    return lax.ppermute(value, ("zl", "zh"), pairs)


def swap_cores(value):
    return lax.ppermute(value, "c", [(0, 1), (1, 0)])


def rotary_tables():
    half = HEAD_SIZE // 2
    positions = jnp.arange(LENGTH, dtype=F32)
    inv_freq = jnp.exp(
        jnp.arange(half, dtype=F32) * (-2.0 * math.log(500000.0) / HEAD_SIZE)
    )
    angles = positions[:, None] * inv_freq[None, :]
    cos, sin = jnp.cos(angles), jnp.sin(angles)
    return jnp.concatenate([cos, cos], axis=1), jnp.concatenate([-sin, sin], axis=1)


def attention_kernel(heads, kept, came, squares, cos_ref, sin_ref, out, total):
    scale = lax.rsqrt(squares[...] * (1.0 / MODEL_WIDTH) + 1e-05)
    cos, sin = cos_ref[...], sin_ref[...]

    def column(i):
        at = slice(i * HEAD_SIZE, (i + 1) * HEAD_SIZE)
        return (kept[:, at] + came[:, at]) * scale

    def rotated(i):
        t = column(i)
        return (t * cos + pltpu.roll(t, HEAD_SIZE // 2, 1) * sin).astype(BF16)

    key, value = rotated(heads), column(heads + 1).astype(BF16)
    row = lax.broadcasted_iota(jnp.int32, (LENGTH, LENGTH), 0)
    causal = row >= lax.broadcasted_iota(jnp.int32, (LENGTH, LENGTH), 1)
    for h in range(heads):
        logits = lax.dot_general(
            rotated(h), key, (((1,), (1,)), ((), ())), preferred_element_type=F32
        )
        logits = jnp.where(causal, logits * (1.0 / math.sqrt(HEAD_SIZE)), -1e30)
        e = jnp.exp(logits - jnp.max(logits, axis=1, keepdims=True))
        probs = (e / jnp.sum(e, axis=1, keepdims=True)).astype(BF16)
        mixed = jnp.dot(probs, value, preferred_element_type=F32).astype(BF16)
        at = slice(h * HEAD_SIZE, (h + 1) * HEAD_SIZE)
        out[:, at] = mixed
        total[:, at] = jnp.sum(mixed.astype(F32), axis=0, keepdims=True)


def attention(heads, kept, came, squares, tables):
    return pl.pallas_call(
        functools.partial(attention_kernel, heads),
        out_shape=(
            jax.ShapeDtypeStruct((LENGTH, heads * HEAD_SIZE), BF16),
            jax.ShapeDtypeStruct((1, heads * HEAD_SIZE), F32),
        ),
        compiler_params=pltpu.CompilerParams(vmem_limit_bytes=24 * 1024 * 1024),
        cost_estimate=pl.CostEstimate(
            flops=4 * heads * LENGTH * LENGTH * HEAD_SIZE,
            bytes_accessed=2 * 4 * LENGTH * 768,
            transcendentals=heads * LENGTH * LENGTH,
        ),
    )(kept, came, squares, *tables)


def ring_share(block):
    cut = block.shape[0] // 2
    own = (block[:cut], block[cut:])
    got = {0: own}
    for sign in (1, -1):
        now = own
        for r in (1, 2, 3):
            now = tuple(along(v, sign) for v in now)
            got[-sign * r] = now
    got[4] = (along(got[-3][0], 1), along(got[3][1], -1))
    return got


def per_device(tokens, gain, w_query, w_key, w_value, w_out, final_gain, unembed, clean, corrupt):
    zh, zl, core = lax.axis_index("zh"), lax.axis_index("zl"), lax.axis_index("c")
    yx = lax.axis_index(("y", "x"))
    first = core == 0
    even = zl % 2 == 0
    width = w_query.shape[1] // 2

    with jax.named_scope("tokens"):
        blocks = ring_share(tokens)

    with jax.named_scope("weights"):
        wkv = jnp.concatenate([w_key, w_value], axis=1)
        upper = zl // 2
        pieces = [
            jnp.concatenate(
                [lax.dynamic_slice_in_dim(w_query, h * width, width, 1), wkv], axis=1
            )
            for h in (upper, 1 - upper)
        ]
        pa = send(pieces[0], lambda z, c: (2 * c + z // 2, z % 2))
        pb = send(pieces[1], lambda z, c: (2 * c + 1 - z // 2, z % 2))
        rows = jnp.concatenate([jnp.where(even, pa, pb), jnp.where(even, pb, pa)], axis=1)
        rows, *_ = lax.optimization_barrier((rows, blocks[1][0], blocks[-1][0]))
        weights = lax.all_gather(rows, ("y", "x"), axis=0, tiled=True)

    with jax.named_scope("direction"):
        vocab_rows = unembed.shape[0]
        ids = lax.axis_index(DP) * vocab_rows + jnp.arange(vocab_rows, dtype=jnp.int32)
        one_hot = (clean[:, None] == ids[None, :]).astype(F32) - (
            corrupt[:, None] == ids[None, :]
        ).astype(F32)
        found = jnp.dot(one_hot.astype(BF16), unembed, preferred_element_type=F32)
        found = found.reshape(4, 16, 16, 128).swapaxes(1, 2).astype(BF16)
        here = (jnp.arange(4) == zl)[:, None, None, None]
        own_last = jnp.where(here, tokens[LENGTH - 1].reshape(1, 16, 1, 128), 0).astype(BF16)
        packed = jnp.concatenate([found, own_last], axis=2).reshape(64, 17, 128)
        packed, *_ = lax.optimization_barrier((packed, blocks[1][1], blocks[-1][1]))
        packed = lax.all_to_all(packed, DP, 0, 0, tiled=True).astype(F32)
        packed = jnp.sum(packed.reshape(4, 16, 17, 128), axis=0)
        gain_cols = lax.dynamic_slice_in_dim(final_gain, yx * 128, 128, 0).astype(F32)
        weighted = gain_cols * jnp.sum(packed[:, :16], axis=0)
        both = jnp.stack([weighted, packed[:, 16]])
        both = from_everyone(both, ("zl", "zh", "c")).reshape(4, 4, 2, 16, 128)
        both = lax.dynamic_index_in_dim(both, zl, 1, keepdims=False)
        weighted_cols = both[:, 0].reshape(64, 128)
        token_cols = both[:, 1].reshape(64, 128)
        back_w = lax.dot_general(
            weighted_cols.astype(BF16), w_out, (((1,), (1,)), ((), ())), preferred_element_type=F32
        )
        grad_w = jnp.sum(lax.all_to_all(back_w[:, None], DP, 0, 0, tiled=True), axis=0)[0]
        other = swap_cores(w_out)
        w_half = jnp.concatenate(
            [jnp.where(first, w_out, other), jnp.where(first, other, w_out)], axis=0
        )

    depth = tokens.shape[1]
    columns = width + 2 * HEAD_SIZE
    heads = width // HEAD_SIZE
    tables = rotary_tables()

    def scaled(k, parts):
        side = ((zh * 4 + zl + k) % 8) // 4
        g = lax.dynamic_slice_in_dim(gain, (2 * side + core) * depth, depth, 0).astype(F32)
        t = jnp.concatenate(parts, axis=0).astype(F32)
        done = ((t * g).astype(BF16), jnp.sum(t * t, axis=1, keepdims=True))
        return (side, *lax.optimization_barrier(done))

    def project(side, block, square):
        weight = lax.dynamic_slice_in_dim(weights, side * columns, columns, 1)
        return jnp.dot(block, weight, preferred_element_type=F32), square

    def both_sides(near, far):
        return tuple(a + b for a, b in zip(near, far))

    def attend(low, high):
        kept = [jnp.where(first, a, b) for a, b in zip(low, high)]
        came = [swap_cores(jnp.where(first, b, a)) for a, b in zip(low, high)]
        return attention(heads, kept[0], came[0], kept[1] + came[1], tables)

    with jax.named_scope("project"):
        known = {k: scaled(k, parts) for k, parts in blocks.items() if k != 4}
        near = project(*known[0])
        next_1, next_2, next_3 = [
            both_sides(project(*known[a]), project(*known[b])) for a, b in ((1, -3), (2, -2), (-1, 3))
        ]
        mixed_1, total_1 = attend(next_1, next_3)
        last_block, near, next_2, mixed_1, grad_w, w_half = lax.optimization_barrier(
            (blocks[4], near, next_2, mixed_1, grad_w, w_half)
        )
        mixed_0, total_0 = attend(both_sides(near, project(*scaled(4, last_block))), next_2)

    with jax.named_scope("return_heads"):
        oa = send(mixed_0, lambda z, c: (z, z // 2) if c == 0 else (z + 2, z // 2))
        ob = send(mixed_1, lambda z, c: (z + 1, z // 2) if c == 0 else (z - 1, z // 2))
        head_out = jnp.concatenate(
            [jnp.where(even, oa, ob), jnp.where(even, ob, oa)], axis=1
        )

    with jax.named_scope("tail"):
        total = total_0 + total_1
        high = lax.reduce_precision(total, 8, 7)
        every = jnp.concatenate(
            [mixed_0[-1:], mixed_1[-1:], high.astype(BF16), (total - high).astype(BF16)], axis=0
        )
        every = from_everyone(every, DP).reshape(4, 16, 4, width)
        total = jnp.sum(every[:, :, 2:].astype(F32), axis=(1, 2)).reshape(16, 128)
        part = jnp.einsum(
            "xpsd,xdn->sxpn", every[:, :, :2], w_half.reshape(4, width, 128), preferred_element_type=F32
        )
        part = jnp.where(
            first,
            part[0] + jnp.roll(part[1], 1, axis=0),
            jnp.roll(part[0], 2, axis=0) + jnp.roll(part[1], -1, axis=0),
        ).reshape(64, 128)
        parts = from_everyone(jnp.concatenate([part, total], axis=0), MP)
        attn_last = jnp.sum(parts[:, :64], axis=0).astype(BF16)
        total = jnp.sum(lax.dynamic_slice_in_dim(parts, 2 * zh, 2, 0)[:, 64:], axis=0)
        head_mean = lax.dynamic_slice_in_dim(total, 8 * core, 8, 0).reshape(1024) / TOKENS
        residual = token_cols + attn_last.astype(F32)
        back_r = lax.dot_general(
            residual.astype(BF16), w_out, (((1,), (1,)), ((), ())), preferred_element_type=F32
        )
        extra = jnp.concatenate(
            [
                jnp.broadcast_to(jnp.sum(residual * residual, axis=1)[:, None], (64, 64)),
                jnp.broadcast_to(jnp.sum(residual * weighted_cols, axis=1)[:, None], (64, 64)),
            ],
            axis=1,
        )
        packed = jnp.concatenate([back_r, extra], axis=1)
        mine = jnp.sum(lax.all_to_all(packed[:, None], DP, 0, 0, tiled=True), axis=0)[0]
        grad_r, square, product = mine[:1024], mine[1024], mine[1024 + 64]
        inverse = lax.rsqrt(square / MODEL_WIDTH + 1e-05)
        metric = inverse * product
        head_grads = grad_w * inverse - grad_r * (metric * inverse * inverse / MODEL_WIDTH)
        last = head_out[LENGTH - 1].astype(F32)
        scores = jnp.sum(((head_mean - last) * head_grads).reshape(1, 8, HEAD_SIZE), axis=2)
    return head_out, scores, metric[None]


def solution(mesh):
    fine = Mesh(mesh.devices.reshape(4, 4, 4, 2, 2), (*DP, *MP))
    in_specs = (
        P(DP, MP),
        P(),
        P(DP, MP),
        P(DP, MP),
        P(DP, MP),
        P(MP, DP),
        P(MP),
        P(DP, MP),
        P(),
        P(),
    )
    out_specs = (P(DP, MP), P(DP, MP), P(DP))
    return jax.shard_map(
        per_device, mesh=fine, in_specs=in_specs, out_specs=out_specs, check_vma=False
    )
```

```python
import functools
import math

import jax
import jax.numpy as jnp
from jax import lax
from jax.experimental import pallas as pl
from jax.experimental.pallas import tpu as pltpu
from jax.sharding import Mesh, PartitionSpec as P

MODEL_WIDTH = 8192
HEAD_SIZE = 128
LENGTH = 256
TOKENS = 16384
DP = ("zl", "y", "x")
MP = ("zh", "c")
F32 = jnp.float32
BF16 = jnp.bfloat16


def from_everyone(value, axis):
    count = lax.axis_size(axis)
    return lax.all_to_all(
        jnp.broadcast_to(value[None], (count, *value.shape)), axis, 0, 0, tiled=True
    )


def send(value, route):
    pairs = []
    for z in range(4):
        for c in range(2):
            to = route(z, c)
            pairs.append((z * 2 + c, (to[0] % 4) * 2 + to[1]))
    return lax.ppermute(value, ("zl", "c"), pairs)


def along(value, step):
    place = lambda z: (z % 4) * 2 + z // 4
    pairs = [(place(z), place((z + step) % 8)) for z in range(8)]
    return lax.ppermute(value, ("zl", "zh"), pairs)


def to_column_owners(value, zl, m):
    got = []
    for i in range(4):
        pairs = [(a * 4 + b, b * 4 + (a + i) % 4) for a in range(4) for b in range(4)]
        got.append(lax.ppermute(value, ("zl", *MP), pairs))
    got = jnp.stack(got)
    return jnp.stack([lax.dynamic_index_in_dim(got, (m - a) % 4, 0, keepdims=False) for a in range(4)])


def sum_over_mp(value):
    others = [
        lax.ppermute(value, MP, [(i, i ^ step) for i in range(4)]).astype(F32) for step in (1, 2, 3)
    ]
    return value.astype(F32) + others[0] + (others[1] + others[2])


def swap_cores(value):
    return lax.ppermute(value, "c", [(0, 1), (1, 0)])


def rotary_tables():
    half = HEAD_SIZE // 2
    positions = jnp.arange(LENGTH, dtype=F32)
    inv_freq = jnp.exp(
        jnp.arange(half, dtype=F32) * (-2.0 * math.log(500000.0) / HEAD_SIZE)
    )
    angles = positions[:, None] * inv_freq[None, :]
    cos, sin = jnp.cos(angles), jnp.sin(angles)
    return jnp.concatenate([cos, cos], axis=1), jnp.concatenate([-sin, sin], axis=1)


def attention_kernel(heads, kept, came, squares, cos_ref, sin_ref, out, total):
    scale = lax.rsqrt(squares[...] * (1.0 / MODEL_WIDTH) + 1e-05)
    cos, sin = cos_ref[...], sin_ref[...]

    def column(i):
        at = slice(i * HEAD_SIZE, (i + 1) * HEAD_SIZE)
        return (kept[:, at] + came[:, at]) * scale

    def rotated(i):
        t = column(i)
        return (t * cos + pltpu.roll(t, HEAD_SIZE // 2, 1) * sin).astype(BF16)

    key, value = rotated(heads), column(heads + 1).astype(BF16)
    row = lax.broadcasted_iota(jnp.int32, (LENGTH, LENGTH), 0)
    causal = row >= lax.broadcasted_iota(jnp.int32, (LENGTH, LENGTH), 1)
    for h in range(heads):
        logits = lax.dot_general(
            rotated(h), key, (((1,), (1,)), ((), ())), preferred_element_type=F32
        )
        logits = jnp.where(causal, logits * (1.0 / math.sqrt(HEAD_SIZE)), -1e30)
        e = jnp.exp(logits - jnp.max(logits, axis=1, keepdims=True))
        probs = (e / jnp.sum(e, axis=1, keepdims=True)).astype(BF16)
        mixed = jnp.dot(probs, value, preferred_element_type=F32).astype(BF16)
        at = slice(h * HEAD_SIZE, (h + 1) * HEAD_SIZE)
        out[:, at] = mixed
        total[:, at] = jnp.sum(mixed.astype(F32), axis=0, keepdims=True)


def attention(heads, kept, came, squares, tables):
    return pl.pallas_call(
        functools.partial(attention_kernel, heads),
        out_shape=(
            jax.ShapeDtypeStruct((LENGTH, heads * HEAD_SIZE), BF16),
            jax.ShapeDtypeStruct((1, heads * HEAD_SIZE), F32),
        ),
        compiler_params=pltpu.CompilerParams(vmem_limit_bytes=24 * 1024 * 1024),
        cost_estimate=pl.CostEstimate(
            flops=4 * heads * LENGTH * LENGTH * HEAD_SIZE,
            bytes_accessed=2 * 4 * LENGTH * 768,
            transcendentals=heads * LENGTH * LENGTH,
        ),
    )(kept, came, squares, *tables)


def ring_share(block):
    got = {0: block}
    for r in (1, 2, 3):
        for sign in (1, -1):
            got[-sign * r] = along(got[-sign * (r - 1)], sign)
    cut = block.shape[0] // 2
    got[4] = (along(got[-3][:cut], 1), along(got[3][cut:], -1))
    return got


def per_device(tokens, gain, w_query, w_key, w_value, w_out, final_gain, unembed, clean, corrupt):
    zh, zl, core = lax.axis_index("zh"), lax.axis_index("zl"), lax.axis_index("c")
    yx = lax.axis_index(("y", "x"))
    first = core == 0

    def back(cols):
        return lax.dot_general(
            cols.astype(BF16), w_out, (((1,), (1,)), ((), ())), preferred_element_type=F32
        )

    even = zl % 2 == 0
    width = w_query.shape[1] // 2

    with jax.named_scope("tokens"):
        blocks = ring_share(tokens)

    with jax.named_scope("weights"):
        wkv = jnp.concatenate([w_key, w_value], axis=1)
        upper = zl // 2
        pieces = [
            jnp.concatenate(
                [lax.dynamic_slice_in_dim(w_query, h * width, width, 1), wkv], axis=1
            )
            for h in (upper, 1 - upper)
        ]
        pa = send(pieces[0], lambda z, c: (2 * c + z // 2, z % 2))
        pb = send(pieces[1], lambda z, c: (2 * c + 1 - z // 2, z % 2))
        rows = jnp.concatenate([jnp.where(even, pa, pb), jnp.where(even, pb, pa)], axis=1)

    with jax.named_scope("direction"):
        vocab_rows = unembed.shape[0]
        ids = lax.axis_index(DP) * vocab_rows + jnp.arange(vocab_rows, dtype=jnp.int32)
        one_hot = (clean[:, None] == ids[None, :]).astype(F32) - (
            corrupt[:, None] == ids[None, :]
        ).astype(F32)
        found = jnp.dot(one_hot.astype(BF16), unembed, preferred_element_type=F32)
        found = found.reshape(4, 16, 16, 128).swapaxes(1, 2).astype(BF16)
        here = (jnp.arange(4) == zl)[:, None, None, None]
        own_last = jnp.where(here, tokens[LENGTH - 1].reshape(1, 16, 1, 128), 0).astype(BF16)
        packed = jnp.concatenate([found, own_last], axis=2).reshape(64, 17, 128)
        packed = lax.all_to_all(packed, DP, 0, 0, tiled=True)
        rows, packed, *_ = lax.optimization_barrier((rows, packed, blocks[1], blocks[-1]))
        weights = lax.all_gather(rows, ("y", "x"), axis=0, tiled=True)
        packed = packed.astype(F32)
        packed = jnp.sum(packed.reshape(4, 16, 17, 128), axis=0)
        gain_cols = lax.dynamic_slice_in_dim(final_gain, yx * 128, 128, 0).astype(F32)
        weighted = gain_cols * jnp.sum(packed[:, :16], axis=0)
        both = jnp.stack([weighted, packed[:, 16]])
        both = to_column_owners(both, zl, 2 * zh + core)
        weighted_cols = both[:, 0].reshape(64, 128)
        token_cols = both[:, 1].reshape(64, 128)
        back_w = back(weighted_cols)

    depth = tokens.shape[1]
    columns = width + 2 * HEAD_SIZE
    heads = width // HEAD_SIZE
    tables = rotary_tables()

    def scaled(k, parts):
        side = ((zh * 4 + zl + k) % 8) // 4
        g = lax.dynamic_slice_in_dim(gain, (2 * side + core) * depth, depth, 0).astype(F32)
        t = parts.astype(F32)
        done = ((t * g).astype(BF16), jnp.sum(t * t, axis=1, keepdims=True))
        return (side, *lax.optimization_barrier(done))

    def project(side, block, square):
        weight = lax.dynamic_slice_in_dim(weights, side * columns, columns, 1)
        return jnp.dot(block, weight, preferred_element_type=F32), square

    def both_sides(near, far):
        return tuple(a + b for a, b in zip(near, far))

    def attend(low, high):
        kept = [jnp.where(first, a, b) for a, b in zip(low, high)]
        came = [swap_cores(jnp.where(first, b, a)) for a, b in zip(low, high)]
        return attention(heads, kept[0], came[0], kept[1] + came[1], tables)

    with jax.named_scope("project"):
        known = {k: scaled(k, parts) for k, parts in blocks.items() if k != 4}
        near = project(*known[0])
        next_1, next_2, next_3 = [
            both_sides(project(*known[a]), project(*known[b])) for a, b in ((1, -3), (2, -2), (-1, 3))
        ]
        mixed_1, total_1 = attend(next_1, next_3)
        last_block, near, next_2, mixed_1, back_w, token_cols = lax.optimization_barrier(
            (blocks[4], near, next_2, mixed_1, back_w, token_cols)
        )
        last_block = project(*scaled(4, jnp.concatenate(last_block, axis=0)))
        mixed_0, total_0 = attend(both_sides(near, last_block), next_2)

    with jax.named_scope("return_heads"):

        def owned(slot_0, slot_1):
            oa = send(slot_0, lambda z, c: (z, z // 2) if c == 0 else (z + 2, z // 2))
            ob = send(slot_1, lambda z, c: (z + 1, z // 2) if c == 0 else (z - 1, z // 2))
            return jnp.concatenate(
                [jnp.where(even, oa, ob), jnp.where(even, ob, oa)], axis=1
            )

        def summary(mixed, total):
            high = lax.reduce_precision(total, 8, 7)
            return jnp.concatenate(
                [mixed[-1:], high.astype(BF16), (total - high).astype(BF16)], axis=0
            )

        own = owned(summary(mixed_0, total_0), summary(mixed_1, total_1))
        own, mixed_0, mixed_1 = lax.optimization_barrier((own, mixed_0, mixed_1))
        head_out = owned(mixed_0, mixed_1)

    with jax.named_scope("tail"):
        every = from_everyone(own, DP)
        last = every[:, 0]
        part = jnp.dot(last, w_out, preferred_element_type=F32).astype(BF16)
        attn_last = sum_over_mp(part).astype(BF16)
        head_mean = jnp.sum(every[:, 1:].astype(F32), axis=(0, 1)) / TOKENS
        gap = head_mean[None] - last.astype(F32)

        def per_head(grads):
            return jnp.sum((gap * grads).reshape(64, 8, HEAD_SIZE), axis=2)

        residual = token_cols + attn_last.astype(F32)
        square = jnp.sum(residual * residual, axis=1, keepdims=True)
        product = jnp.sum(residual * weighted_cols, axis=1, keepdims=True)
        packed = jnp.concatenate(
            [
                per_head(back_w),
                per_head(back(residual)),
                jnp.broadcast_to(square, (64, 56)),
                jnp.broadcast_to(product, (64, 56)),
            ],
            axis=1,
        )
        mine = jnp.sum(lax.all_to_all(packed[:, None], DP, 0, 0, tiled=True), axis=0)
        inverse = lax.rsqrt(mine[:, 16] / MODEL_WIDTH + 1e-05)
        metric = inverse * mine[:, 72]
        scores = inverse * mine[:, :8] - (metric * inverse * inverse / MODEL_WIDTH) * mine[:, 8:16]
    return head_out, scores, metric


def solution(mesh):
    fine = Mesh(mesh.devices.reshape(4, 4, 4, 2, 2), (*DP, *MP))
    in_specs = (
        P(DP, MP),
        P(),
        P(DP, MP),
        P(DP, MP),
        P(DP, MP),
        P(MP, DP),
        P(MP),
        P(DP, MP),
        P(),
        P(),
    )
    out_specs = (P(DP, MP), P(DP, MP), P(DP))
    return jax.shard_map(
        per_device, mesh=fine, in_specs=in_specs, out_specs=out_specs, check_vma=False
    )
```

```python
import functools
import math

import jax
import jax.numpy as jnp
from jax import lax
from jax.experimental import pallas as pl
from jax.experimental.pallas import tpu as pltpu
from jax.sharding import Mesh, PartitionSpec as P

MODEL_WIDTH = 8192
HEAD_SIZE = 128
LENGTH = 256
TOKENS = 16384
DP = ("zl", "y", "x")
MP = ("zh", "c")
F32 = jnp.float32
BF16 = jnp.bfloat16


def from_everyone(value, axis):
    count = lax.axis_size(axis)
    return lax.all_to_all(
        jnp.broadcast_to(value[None], (count, *value.shape)), axis, 0, 0, tiled=True
    )


def send(value, route):
    pairs = []
    for z in range(4):
        for c in range(2):
            to = route(z, c)
            pairs.append((z * 2 + c, (to[0] % 4) * 2 + to[1]))
    return lax.ppermute(value, ("zl", "c"), pairs)


def along(value, step):
    place = lambda z: (z % 4) * 2 + z // 4
    pairs = [(place(z), place((z + step) % 8)) for z in range(8)]
    return lax.ppermute(value, ("zl", "zh"), pairs)


def to_column_owners(value, zl, m):
    got = []
    for i in range(4):
        pairs = [(a * 4 + b, b * 4 + (a + i) % 4) for a in range(4) for b in range(4)]
        got.append(lax.ppermute(value, ("zl", *MP), pairs))
    got = jnp.stack(got)
    return jnp.stack([lax.dynamic_index_in_dim(got, (m - a) % 4, 0, keepdims=False) for a in range(4)])


def sum_over_mp(value):
    others = [
        lax.ppermute(value, MP, [(i, i ^ step) for i in range(4)]).astype(F32) for step in (1, 2, 3)
    ]
    return value.astype(F32) + others[0] + (others[1] + others[2])


def swap_cores(value):
    return lax.ppermute(value, "c", [(0, 1), (1, 0)])


def rotary_tables():
    half = HEAD_SIZE // 2
    positions = jnp.arange(LENGTH, dtype=F32)
    inv_freq = jnp.exp(
        jnp.arange(half, dtype=F32) * (-2.0 * math.log(500000.0) / HEAD_SIZE)
    )
    angles = positions[:, None] * inv_freq[None, :]
    cos, sin = jnp.cos(angles), jnp.sin(angles)
    return jnp.concatenate([cos, cos], axis=1), jnp.concatenate([-sin, sin], axis=1)


def attention_kernel(heads, kept, came, squares, cos_ref, sin_ref, out, total):
    scale = lax.rsqrt(squares[...] * (1.0 / MODEL_WIDTH) + 1e-05)
    cos, sin = cos_ref[...], sin_ref[...]

    def column(i):
        at = slice(i * HEAD_SIZE, (i + 1) * HEAD_SIZE)
        return (kept[:, at] + came[:, at]) * scale

    def rotated(i):
        t = column(i)
        return (t * cos + pltpu.roll(t, HEAD_SIZE // 2, 1) * sin).astype(BF16)

    key, value = rotated(heads), column(heads + 1).astype(BF16)
    row = lax.broadcasted_iota(jnp.int32, (LENGTH, LENGTH), 0)
    causal = row >= lax.broadcasted_iota(jnp.int32, (LENGTH, LENGTH), 1)
    for h in range(heads):
        logits = lax.dot_general(
            rotated(h), key, (((1,), (1,)), ((), ())), preferred_element_type=F32
        )
        logits = jnp.where(causal, logits * (1.0 / math.sqrt(HEAD_SIZE)), -1e30)
        e = jnp.exp(logits - jnp.max(logits, axis=1, keepdims=True))
        probs = (e / jnp.sum(e, axis=1, keepdims=True)).astype(BF16)
        mixed = jnp.dot(probs, value, preferred_element_type=F32).astype(BF16)
        at = slice(h * HEAD_SIZE, (h + 1) * HEAD_SIZE)
        out[:, at] = mixed
        total[:, at] = jnp.sum(mixed.astype(F32), axis=0, keepdims=True)


def attention(heads, kept, came, squares, tables):
    return pl.pallas_call(
        functools.partial(attention_kernel, heads),
        out_shape=(
            jax.ShapeDtypeStruct((LENGTH, heads * HEAD_SIZE), BF16),
            jax.ShapeDtypeStruct((1, heads * HEAD_SIZE), F32),
        ),
        compiler_params=pltpu.CompilerParams(vmem_limit_bytes=24 * 1024 * 1024),
        cost_estimate=pl.CostEstimate(
            flops=4 * heads * LENGTH * LENGTH * HEAD_SIZE,
            bytes_accessed=2 * 4 * LENGTH * 768,
            transcendentals=heads * LENGTH * LENGTH,
        ),
    )(kept, came, squares, *tables)


def last_hop(value):
    place = lambda z, c: (z % 4) * 4 + (z // 4) * 2 + c
    pairs = [
        (place(z, c), place((z + 1 - 2 * c) % 8, c)) for z in range(8) for c in range(2)
    ]
    return lax.ppermute(value, ("zl", *MP), pairs)


def to_line(value, zl):
    got = []
    for i in range(4):
        got.append(send(value, lambda z, c: (2 * (z % 2) + c + i, z // 2)))
    got = jnp.stack(got)
    return jnp.stack(
        [lax.dynamic_index_in_dim(got, (zl - q) % 4, 0, keepdims=False) for q in range(4)]
    )


def per_device(tokens, gain, w_query, w_key, w_value, w_out, final_gain, unembed, clean, corrupt):
    zh, zl, core = lax.axis_index("zh"), lax.axis_index("zl"), lax.axis_index("c")
    yx = lax.axis_index(("y", "x"))
    first = core == 0

    def back(cols):
        return lax.dot_general(
            cols.astype(BF16), w_out, (((1,), (1,)), ((), ())), preferred_element_type=F32
        )

    even = zl % 2 == 0
    width = w_query.shape[1] // 2

    with jax.named_scope("weights"):
        wkv = jnp.concatenate([w_key, w_value], axis=1)
        upper = zl // 2
        pieces = [
            jnp.concatenate(
                [lax.dynamic_slice_in_dim(w_query, h * width, width, 1), wkv], axis=1
            )
            for h in (upper, 1 - upper)
        ]
        pa = send(pieces[0], lambda z, c: (2 * c + z // 2, z % 2))
        pb = send(pieces[1], lambda z, c: (2 * c + 1 - z // 2, z % 2))
        rows = jnp.concatenate([jnp.where(even, pa, pb), jnp.where(even, pb, pa)], axis=1)
        weights = lax.all_gather(rows, ("y", "x"), axis=0, tiled=True)

    with jax.named_scope("direction"):
        vocab_rows = unembed.shape[0]
        ids = lax.axis_index(DP) * vocab_rows + jnp.arange(vocab_rows, dtype=jnp.int32)
        one_hot = (clean[:, None] == ids[None, :]).astype(F32) - (
            corrupt[:, None] == ids[None, :]
        ).astype(F32)
        found = jnp.dot(one_hot.astype(BF16), unembed, preferred_element_type=F32)
        found = found.reshape(4, 16, 16, 128).swapaxes(1, 2).astype(BF16)
        here = (jnp.arange(4) == zl)[:, None, None, None]
        own_last = jnp.where(here, tokens[LENGTH - 1].reshape(1, 16, 1, 128), 0).astype(BF16)
        packed = jnp.concatenate([found, own_last], axis=2).reshape(64, 17, 128)
        packed = lax.all_to_all(packed, DP, 0, 0, tiled=True)
        packed = packed.astype(F32)
        packed = jnp.sum(packed.reshape(4, 16, 17, 128), axis=0)
        gain_cols = lax.dynamic_slice_in_dim(final_gain, yx * 128, 128, 0).astype(F32)
        weighted = gain_cols * jnp.sum(packed[:, :16], axis=0)
        both = jnp.stack([weighted, packed[:, 16]])
        both = to_column_owners(both, zl, 2 * zh + core)
        blocks = {0: tokens}
        for r in (1, 2, 3):
            for sign in (1, -1):
                blocks[-sign * r] = along(blocks[-sign * (r - 1)], sign)
            if r == 2:
                both, blocks[2], blocks[-2] = lax.optimization_barrier(
                    (both, blocks[2], blocks[-2])
                )
        blocks[4] = last_hop(jnp.where(first, blocks[-3], blocks[3]))
        weighted_cols = both[:, 0].reshape(64, 128)
        token_cols = both[:, 1].reshape(64, 128)
        back_w = back(weighted_cols)

    depth = tokens.shape[1]
    columns = width + 2 * HEAD_SIZE
    heads = width // HEAD_SIZE
    tables = rotary_tables()

    def scaled(k, parts):
        side = ((zh * 4 + zl + k) % 8) // 4
        g = lax.dynamic_slice_in_dim(gain, (2 * side + core) * depth, depth, 0).astype(F32)
        t = parts.astype(F32)
        done = ((t * g).astype(BF16), jnp.sum(t * t, axis=1, keepdims=True))
        return (side, *lax.optimization_barrier(done))

    def project(side, block, square):
        weight = lax.dynamic_slice_in_dim(weights, side * columns, columns, 1)
        return jnp.dot(block, weight, preferred_element_type=F32), square

    def both_sides(near, far):
        return tuple(a + b for a, b in zip(near, far))

    def attend(low, high):
        kept = [jnp.where(first, a, b) for a, b in zip(low, high)]
        came = [swap_cores(jnp.where(first, b, a)) for a, b in zip(low, high)]
        return attention(heads, kept[0], came[0], kept[1] + came[1], tables)

    with jax.named_scope("project"):
        known = {k: scaled(k, parts) for k, parts in blocks.items() if k != 4}
        near = project(*known[0])
        next_1, next_2, next_3 = [
            both_sides(project(*known[a]), project(*known[b])) for a, b in ((1, -3), (2, -2), (-1, 3))
        ]
        mixed_1, total_1 = attend(next_1, next_3)
        last_block, near, next_2, mixed_1, back_w, token_cols = lax.optimization_barrier(
            (blocks[4], near, next_2, mixed_1, back_w, token_cols)
        )
        last_block = project(*scaled(4, last_block))
        mixed_0, total_0 = attend(both_sides(near, last_block), next_2)

    with jax.named_scope("return_heads"):

        def owned(slot_0, slot_1):
            oa = send(slot_0, lambda z, c: (z, z // 2) if c == 0 else (z + 2, z // 2))
            ob = send(slot_1, lambda z, c: (z + 1, z // 2) if c == 0 else (z - 1, z // 2))
            return jnp.concatenate(
                [jnp.where(even, oa, ob), jnp.where(even, ob, oa)], axis=1
            )

    with jax.named_scope("tail"):
        total = total_0 + total_1
        high = lax.reduce_precision(total, 8, 7)
        line = jnp.concatenate(
            [mixed_0[-1:], mixed_1[-1:], high.astype(BF16), (total - high).astype(BF16)], axis=0
        )
        every = from_everyone(to_line(line, zl), ("y", "x"))
        every, mixed_0, mixed_1 = lax.optimization_barrier((every, mixed_0, mixed_1))
        head_out = owned(mixed_0, mixed_1)
        every = every.reshape(16, 2, 2, 4, width)
        last = every[:, :, :, :2].reshape(16, 2, 4, width)
        last = jnp.concatenate(
            [
                jnp.where(first, jnp.roll(last[:, h], h, axis=1), jnp.roll(last[:, h], h + 2, axis=1))
                for h in (0, 1)
            ],
            axis=2,
        )
        last = last.swapaxes(0, 1).reshape(64, 2 * width)
        part = jnp.dot(last, w_out, preferred_element_type=F32).astype(BF16)
        attn_last = sum_over_mp(part).astype(BF16)
        head_mean = jnp.sum(every[:, :, :, 2:].astype(F32), axis=(0, 2, 3)).reshape(-1) / TOKENS
        gap = head_mean[None] - last.astype(F32)

        def per_head(grads):
            return jnp.sum((gap * grads).reshape(64, 8, HEAD_SIZE), axis=2)

        residual = token_cols + attn_last.astype(F32)
        square = jnp.sum(residual * residual, axis=1, keepdims=True)
        product = jnp.sum(residual * weighted_cols, axis=1, keepdims=True)
        packed = jnp.concatenate(
            [
                per_head(back_w),
                per_head(back(residual)),
                jnp.broadcast_to(square, (64, 56)),
                jnp.broadcast_to(product, (64, 56)),
            ],
            axis=1,
        )
        mine = jnp.sum(lax.all_to_all(packed[:, None], DP, 0, 0, tiled=True), axis=0)
        inverse = lax.rsqrt(mine[:, 16] / MODEL_WIDTH + 1e-05)
        metric = inverse * mine[:, 72]
        scores = inverse * mine[:, :8] - (metric * inverse * inverse / MODEL_WIDTH) * mine[:, 8:16]
    return head_out, scores, metric


def solution(mesh):
    fine = Mesh(mesh.devices.reshape(4, 4, 4, 2, 2), (*DP, *MP))
    in_specs = (
        P(DP, MP),
        P(),
        P(DP, MP),
        P(DP, MP),
        P(DP, MP),
        P(MP, DP),
        P(MP),
        P(DP, MP),
        P(),
        P(),
    )
    out_specs = (P(DP, MP), P(DP, MP), P(DP))
    return jax.shard_map(
        per_device, mesh=fine, in_specs=in_specs, out_specs=out_specs, check_vma=False
    )
```

```python
import functools
import math

import jax
import jax.numpy as jnp
from jax import lax
from jax.experimental import pallas as pl
from jax.experimental.pallas import tpu as pltpu
from jax.sharding import Mesh, PartitionSpec as P

MODEL_WIDTH = 8192
HEAD_SIZE = 128
LENGTH = 256
TOKENS = 16384
DP = ("zl", "y", "x")
MP = ("zh", "c")
F32 = jnp.float32
BF16 = jnp.bfloat16


def from_everyone(value, axis):
    count = lax.axis_size(axis)
    return lax.all_to_all(
        jnp.broadcast_to(value[None], (count, *value.shape)), axis, 0, 0, tiled=True
    )


def send(value, route):
    pairs = []
    for z in range(4):
        for c in range(2):
            to = route(z, c)
            pairs.append((z * 2 + c, (to[0] % 4) * 2 + to[1]))
    return lax.ppermute(value, ("zl", "c"), pairs)


def along(value, step):
    place = lambda z: (z % 4) * 2 + z // 4
    pairs = [(place(z), place((z + step) % 8)) for z in range(8)]
    return lax.ppermute(value, ("zl", "zh"), pairs)


def to_column_owners(value, zl, m):
    got = []
    for i in range(4):
        pairs = [(a * 4 + b, b * 4 + (a + i) % 4) for a in range(4) for b in range(4)]
        got.append(lax.ppermute(value, ("zl", *MP), pairs))
    got = jnp.stack(got)
    return jnp.stack([lax.dynamic_index_in_dim(got, (m - a) % 4, 0, keepdims=False) for a in range(4)])


def sum_over_mp(value):
    others = [
        lax.ppermute(value, MP, [(i, i ^ step) for i in range(4)]).astype(F32) for step in (1, 2, 3)
    ]
    return value.astype(F32) + others[0] + (others[1] + others[2])


def swap_cores(value):
    return lax.ppermute(value, "c", [(0, 1), (1, 0)])


def rotary_tables():
    half = HEAD_SIZE // 2
    positions = jnp.arange(LENGTH, dtype=F32)
    inv_freq = jnp.exp(
        jnp.arange(half, dtype=F32) * (-2.0 * math.log(500000.0) / HEAD_SIZE)
    )
    angles = positions[:, None] * inv_freq[None, :]
    cos, sin = jnp.cos(angles), jnp.sin(angles)
    return jnp.concatenate([cos, cos], axis=1), jnp.concatenate([-sin, sin], axis=1)


def attention_kernel(heads, kept, came, squares, cos_ref, sin_ref, out, total):
    scale = lax.rsqrt(squares[...] * (1.0 / MODEL_WIDTH) + 1e-05)
    cos, sin = cos_ref[...], sin_ref[...]

    def column(i):
        at = slice(i * HEAD_SIZE, (i + 1) * HEAD_SIZE)
        return (kept[:, at] + came[:, at]) * scale

    def rotated(i):
        t = column(i)
        return (t * cos + pltpu.roll(t, HEAD_SIZE // 2, 1) * sin).astype(BF16)

    key, value = rotated(heads), column(heads + 1).astype(BF16)
    row = lax.broadcasted_iota(jnp.int32, (LENGTH, LENGTH), 0)
    causal = row >= lax.broadcasted_iota(jnp.int32, (LENGTH, LENGTH), 1)
    for h in range(heads):
        logits = lax.dot_general(
            rotated(h), key, (((1,), (1,)), ((), ())), preferred_element_type=F32
        )
        logits = jnp.where(causal, logits * (1.0 / math.sqrt(HEAD_SIZE)), -1e30)
        e = jnp.exp(logits - jnp.max(logits, axis=1, keepdims=True))
        probs = (e / jnp.sum(e, axis=1, keepdims=True)).astype(BF16)
        mixed = jnp.dot(probs, value, preferred_element_type=F32).astype(BF16)
        at = slice(h * HEAD_SIZE, (h + 1) * HEAD_SIZE)
        out[:, at] = mixed
        total[:, at] = jnp.sum(mixed.astype(F32), axis=0, keepdims=True)


def attention(heads, kept, came, squares, tables):
    return pl.pallas_call(
        functools.partial(attention_kernel, heads),
        out_shape=(
            jax.ShapeDtypeStruct((LENGTH, heads * HEAD_SIZE), BF16),
            jax.ShapeDtypeStruct((1, heads * HEAD_SIZE), F32),
        ),
        compiler_params=pltpu.CompilerParams(vmem_limit_bytes=24 * 1024 * 1024),
        cost_estimate=pl.CostEstimate(
            flops=4 * heads * LENGTH * LENGTH * HEAD_SIZE,
            bytes_accessed=2 * 4 * LENGTH * 768,
            transcendentals=heads * LENGTH * LENGTH,
        ),
    )(kept, came, squares, *tables)


def last_hop(value):
    place = lambda z, c: (z % 4) * 4 + (z // 4) * 2 + c
    pairs = [
        (place(z, c), place((z + 1 - 2 * c) % 8, c)) for z in range(8) for c in range(2)
    ]
    return lax.ppermute(value, ("zl", *MP), pairs)


def per_device(tokens, gain, w_query, w_key, w_value, w_out, final_gain, unembed, clean, corrupt):
    zh, zl, core = lax.axis_index("zh"), lax.axis_index("zl"), lax.axis_index("c")
    yx = lax.axis_index(("y", "x"))
    first = core == 0

    def back(cols):
        return lax.dot_general(
            cols.astype(BF16), w_out, (((1,), (1,)), ((), ())), preferred_element_type=F32
        )

    even = zl % 2 == 0
    width = w_query.shape[1] // 2

    with jax.named_scope("weights"):
        wkv = jnp.concatenate([w_key, w_value], axis=1)
        upper = zl // 2
        pieces = [
            jnp.concatenate(
                [lax.dynamic_slice_in_dim(w_query, h * width, width, 1), wkv], axis=1
            )
            for h in (upper, 1 - upper)
        ]
        pa = send(pieces[0], lambda z, c: (2 * c + z // 2, z % 2))
        pb = send(pieces[1], lambda z, c: (2 * c + 1 - z // 2, z % 2))
        rows = jnp.concatenate([jnp.where(even, pa, pb), jnp.where(even, pb, pa)], axis=1)
        weights = lax.all_gather(rows, ("y", "x"), axis=0, tiled=True)

    with jax.named_scope("direction"):
        vocab_rows = unembed.shape[0]
        ids = lax.axis_index(DP) * vocab_rows + jnp.arange(vocab_rows, dtype=jnp.int32)
        one_hot = (clean[:, None] == ids[None, :]).astype(F32) - (
            corrupt[:, None] == ids[None, :]
        ).astype(F32)
        found = jnp.dot(one_hot.astype(BF16), unembed, preferred_element_type=F32)
        found = found.reshape(4, 16, 16, 128).swapaxes(1, 2).astype(BF16)
        here = (jnp.arange(4) == zl)[:, None, None, None]
        own_last = jnp.where(here, tokens[LENGTH - 1].reshape(1, 16, 1, 128), 0).astype(BF16)
        packed = jnp.concatenate([found, own_last], axis=2).reshape(64, 17, 128)
        packed = lax.all_to_all(packed, DP, 0, 0, tiled=True)
        blocks = {0: tokens}
        for r in (1, 2, 3):
            for sign in (1, -1):
                blocks[-sign * r] = along(blocks[-sign * (r - 1)], sign)
            if r == 2:
                packed, *_ = lax.optimization_barrier((packed, blocks[2], blocks[-2]))
        packed = packed.astype(F32)
        packed = jnp.sum(packed.reshape(4, 16, 17, 128), axis=0)
        gain_cols = lax.dynamic_slice_in_dim(final_gain, yx * 128, 128, 0).astype(F32)
        weighted = gain_cols * jnp.sum(packed[:, :16], axis=0)
        both = jnp.stack([weighted, packed[:, 16]])
        both = to_column_owners(both, zl, 2 * zh + core)
        both, blocks[3], blocks[-3] = lax.optimization_barrier((both, blocks[3], blocks[-3]))
        blocks[4] = last_hop(jnp.where(first, blocks[-3], blocks[3]))
        weighted_cols = both[:, 0].reshape(64, 128)
        token_cols = both[:, 1].reshape(64, 128)
        back_w = back(weighted_cols)

    depth = tokens.shape[1]
    columns = width + 2 * HEAD_SIZE
    heads = width // HEAD_SIZE
    tables = rotary_tables()

    def scaled(k, parts):
        side = ((zh * 4 + zl + k) % 8) // 4
        g = lax.dynamic_slice_in_dim(gain, (2 * side + core) * depth, depth, 0).astype(F32)
        t = parts.astype(F32)
        done = ((t * g).astype(BF16), jnp.sum(t * t, axis=1, keepdims=True))
        return (side, *lax.optimization_barrier(done))

    def project(side, block, square):
        weight = lax.dynamic_slice_in_dim(weights, side * columns, columns, 1)
        return jnp.dot(block, weight, preferred_element_type=F32), square

    def both_sides(near, far):
        return tuple(a + b for a, b in zip(near, far))

    def attend(low, high):
        kept = [jnp.where(first, a, b) for a, b in zip(low, high)]
        came = [swap_cores(jnp.where(first, b, a)) for a, b in zip(low, high)]
        return attention(heads, kept[0], came[0], kept[1] + came[1], tables)

    with jax.named_scope("project"):
        known = {k: scaled(k, parts) for k, parts in blocks.items() if k != 4}
        near = project(*known[0])
        next_1, next_2, next_3 = [
            both_sides(project(*known[a]), project(*known[b])) for a, b in ((1, -3), (2, -2), (-1, 3))
        ]
        mixed_1, total_1 = attend(next_1, next_3)
        last_block, near, next_2, mixed_1, back_w, token_cols = lax.optimization_barrier(
            (blocks[4], near, next_2, mixed_1, back_w, token_cols)
        )
        last_block = project(*scaled(4, last_block))
        mixed_0, total_0 = attend(both_sides(near, last_block), next_2)

    with jax.named_scope("return_heads"):

        def owned(slot_0, slot_1):
            oa = send(slot_0, lambda z, c: (z, z // 2) if c == 0 else (z + 2, z // 2))
            ob = send(slot_1, lambda z, c: (z + 1, z // 2) if c == 0 else (z - 1, z // 2))
            return jnp.concatenate(
                [jnp.where(even, oa, ob), jnp.where(even, ob, oa)], axis=1
            )

    with jax.named_scope("tail"):
        total = total_0 + total_1
        high = lax.reduce_precision(total, 8, 7)
        line = jnp.concatenate(
            [mixed_0[-1:], mixed_1[-1:], high.astype(BF16), (total - high).astype(BF16)], axis=0
        )
        line = lax.dynamic_slice_in_dim(from_everyone(line, ("zl", "c")), 4 * core, 4, 0)
        every = from_everyone(line, ("y", "x"))
        every, mixed_0, mixed_1 = lax.optimization_barrier((every, mixed_0, mixed_1))
        head_out = owned(mixed_0, mixed_1)
        every = every.reshape(16, 2, 2, 4, width)
        last = every[:, :, :, :2].reshape(16, 2, 4, width)
        last = jnp.concatenate(
            [
                jnp.where(first, jnp.roll(last[:, h], h, axis=1), jnp.roll(last[:, h], h + 2, axis=1))
                for h in (0, 1)
            ],
            axis=2,
        )
        last = last.swapaxes(0, 1).reshape(64, 2 * width)
        part = jnp.dot(last, w_out, preferred_element_type=F32).astype(BF16)
        attn_last = sum_over_mp(part).astype(BF16)
        head_mean = jnp.sum(every[:, :, :, 2:].astype(F32), axis=(0, 2, 3)).reshape(-1) / TOKENS
        gap = head_mean[None] - last.astype(F32)

        def per_head(grads):
            return jnp.sum((gap * grads).reshape(64, 8, HEAD_SIZE), axis=2)

        residual = token_cols + attn_last.astype(F32)
        square = jnp.sum(residual * residual, axis=1, keepdims=True)
        product = jnp.sum(residual * weighted_cols, axis=1, keepdims=True)
        packed = jnp.concatenate(
            [
                per_head(back_w),
                per_head(back(residual)),
                jnp.broadcast_to(square, (64, 56)),
                jnp.broadcast_to(product, (64, 56)),
            ],
            axis=1,
        )
        mine = jnp.sum(lax.all_to_all(packed[:, None], DP, 0, 0, tiled=True), axis=0)
        inverse = lax.rsqrt(mine[:, 16] / MODEL_WIDTH + 1e-05)
        metric = inverse * mine[:, 72]
        scores = inverse * mine[:, :8] - (metric * inverse * inverse / MODEL_WIDTH) * mine[:, 8:16]
    return head_out, scores, metric


def solution(mesh):
    fine = Mesh(mesh.devices.reshape(4, 4, 4, 2, 2), (*DP, *MP))
    in_specs = (
        P(DP, MP),
        P(),
        P(DP, MP),
        P(DP, MP),
        P(DP, MP),
        P(MP, DP),
        P(MP),
        P(DP, MP),
        P(),
        P(),
    )
    out_specs = (P(DP, MP), P(DP, MP), P(DP))
    return jax.shard_map(
        per_device, mesh=fine, in_specs=in_specs, out_specs=out_specs, check_vma=False
    )
```

```python
import functools
import math

import jax
import jax.numpy as jnp
from jax import lax
from jax.experimental import pallas as pl
from jax.experimental.pallas import tpu as pltpu
from jax.sharding import Mesh, PartitionSpec as P

MODEL_WIDTH = 8192
HEAD_SIZE = 128
LENGTH = 256
TOKENS = 16384
DP = ("zl", "y", "x")
MP = ("zh", "c")
F32 = jnp.float32
BF16 = jnp.bfloat16


def from_everyone(value, axis):
    count = lax.axis_size(axis)
    return lax.all_to_all(
        jnp.broadcast_to(value[None], (count, *value.shape)), axis, 0, 0, tiled=True
    )


def send(value, route):
    pairs = []
    for z in range(4):
        for c in range(2):
            to = route(z, c)
            pairs.append((z * 2 + c, (to[0] % 4) * 2 + to[1]))
    return lax.ppermute(value, ("zl", "c"), pairs)


def along(value, step):
    place = lambda z: (z % 4) * 2 + z // 4
    pairs = [(place(z), place((z + step) % 8)) for z in range(8)]
    return lax.ppermute(value, ("zl", "zh"), pairs)


def to_column_owners(value, zl, m):
    got = []
    for i in range(4):
        pairs = [(a * 4 + b, b * 4 + (a + i) % 4) for a in range(4) for b in range(4)]
        got.append(lax.ppermute(value, ("zl", *MP), pairs))
    got = jnp.stack(got)
    return jnp.stack([lax.dynamic_index_in_dim(got, (m - a) % 4, 0, keepdims=False) for a in range(4)])


def sum_over_mp(value):
    others = [
        lax.ppermute(value, MP, [(i, i ^ step) for i in range(4)]).astype(F32) for step in (1, 2, 3)
    ]
    return value.astype(F32) + others[0] + (others[1] + others[2])


def swap_cores(value):
    return lax.ppermute(value, "c", [(0, 1), (1, 0)])


def rotary_tables():
    half = HEAD_SIZE // 2
    positions = jnp.arange(LENGTH, dtype=F32)
    inv_freq = jnp.exp(
        jnp.arange(half, dtype=F32) * (-2.0 * math.log(500000.0) / HEAD_SIZE)
    )
    angles = positions[:, None] * inv_freq[None, :]
    cos, sin = jnp.cos(angles), jnp.sin(angles)
    return jnp.concatenate([cos, cos], axis=1), jnp.concatenate([-sin, sin], axis=1)


def attention_kernel(heads, kept, came, squares, cos_ref, sin_ref, out, total):
    scale = lax.rsqrt(squares[...] * (1.0 / MODEL_WIDTH) + 1e-05)
    cos, sin = cos_ref[...], sin_ref[...]

    def column(i):
        at = slice(i * HEAD_SIZE, (i + 1) * HEAD_SIZE)
        return (kept[:, at] + came[:, at]) * scale

    def rotated(i):
        t = column(i)
        return (t * cos + pltpu.roll(t, HEAD_SIZE // 2, 1) * sin).astype(BF16)

    key, value = rotated(heads), column(heads + 1).astype(BF16)
    row = lax.broadcasted_iota(jnp.int32, (LENGTH, LENGTH), 0)
    causal = row >= lax.broadcasted_iota(jnp.int32, (LENGTH, LENGTH), 1)
    for h in range(heads):
        logits = lax.dot_general(
            rotated(h), key, (((1,), (1,)), ((), ())), preferred_element_type=F32
        )
        logits = jnp.where(causal, logits * (1.0 / math.sqrt(HEAD_SIZE)), -1e30)
        e = jnp.exp(logits - jnp.max(logits, axis=1, keepdims=True))
        probs = (e / jnp.sum(e, axis=1, keepdims=True)).astype(BF16)
        mixed = jnp.dot(probs, value, preferred_element_type=F32).astype(BF16)
        at = slice(h * HEAD_SIZE, (h + 1) * HEAD_SIZE)
        out[:, at] = mixed
        total[:, at] = jnp.sum(mixed.astype(F32), axis=0, keepdims=True)


def attention(heads, kept, came, squares, tables):
    return pl.pallas_call(
        functools.partial(attention_kernel, heads),
        out_shape=(
            jax.ShapeDtypeStruct((LENGTH, heads * HEAD_SIZE), BF16),
            jax.ShapeDtypeStruct((1, heads * HEAD_SIZE), F32),
        ),
        compiler_params=pltpu.CompilerParams(vmem_limit_bytes=24 * 1024 * 1024),
        cost_estimate=pl.CostEstimate(
            flops=4 * heads * LENGTH * LENGTH * HEAD_SIZE,
            bytes_accessed=2 * 4 * LENGTH * 768,
            transcendentals=heads * LENGTH * LENGTH,
        ),
    )(kept, came, squares, *tables)


def last_hop(value):
    place = lambda z, c: (z % 4) * 4 + (z // 4) * 2 + c
    pairs = [
        (place(z, c), place((z + 1 - 2 * c) % 8, c)) for z in range(8) for c in range(2)
    ]
    return lax.ppermute(value, ("zl", *MP), pairs)


def per_device(tokens, gain, w_query, w_key, w_value, w_out, final_gain, unembed, clean, corrupt):
    zh, zl, core = lax.axis_index("zh"), lax.axis_index("zl"), lax.axis_index("c")
    yx = lax.axis_index(("y", "x"))
    first = core == 0

    def back(cols):
        return lax.dot_general(
            cols.astype(BF16), w_out, (((1,), (1,)), ((), ())), preferred_element_type=F32
        )

    even = zl % 2 == 0
    width = w_query.shape[1] // 2

    with jax.named_scope("weights"):
        wkv = jnp.concatenate([w_key, w_value], axis=1)
        upper = zl // 2
        pieces = [
            jnp.concatenate(
                [lax.dynamic_slice_in_dim(w_query, h * width, width, 1), wkv], axis=1
            )
            for h in (upper, 1 - upper)
        ]
        pa = send(pieces[0], lambda z, c: (2 * c + z // 2, z % 2))
        pb = send(pieces[1], lambda z, c: (2 * c + 1 - z // 2, z % 2))
        rows = jnp.concatenate([jnp.where(even, pa, pb), jnp.where(even, pb, pa)], axis=1)
        weights = lax.all_gather(rows, ("y", "x"), axis=0, tiled=True)

    with jax.named_scope("direction"):
        vocab_rows = unembed.shape[0]
        ids = lax.axis_index(DP) * vocab_rows + jnp.arange(vocab_rows, dtype=jnp.int32)
        one_hot = (clean[:, None] == ids[None, :]).astype(F32) - (
            corrupt[:, None] == ids[None, :]
        ).astype(F32)
        found = jnp.dot(one_hot.astype(BF16), unembed, preferred_element_type=F32)
        found = found.reshape(4, 16, 16, 128).swapaxes(1, 2).astype(BF16)
        here = (jnp.arange(4) == zl)[:, None, None, None]
        own_last = jnp.where(here, tokens[LENGTH - 1].reshape(1, 16, 1, 128), 0).astype(BF16)
        packed = jnp.concatenate([found, own_last], axis=2).reshape(64, 17, 128)
        packed = lax.all_to_all(packed, DP, 0, 0, tiled=True)
        blocks = {0: tokens}
        for r in (1, 2, 3):
            for sign in (1, -1):
                blocks[-sign * r] = along(blocks[-sign * (r - 1)], sign)
            if r == 2:
                packed, *_ = lax.optimization_barrier((packed, blocks[2], blocks[-2]))
        packed = packed.astype(F32)
        packed = jnp.sum(packed.reshape(4, 16, 17, 128), axis=0)
        gain_cols = lax.dynamic_slice_in_dim(final_gain, yx * 128, 128, 0).astype(F32)
        weighted = gain_cols * jnp.sum(packed[:, :16], axis=0)
        both = jnp.stack([weighted, packed[:, 16]])
        both, weights = lax.optimization_barrier((both, weights))
        both = to_column_owners(both, zl, 2 * zh + core)

    depth = tokens.shape[1]
    columns = width + 2 * HEAD_SIZE
    heads = width // HEAD_SIZE
    tables = rotary_tables()

    def scaled(k, parts):
        side = ((zh * 4 + zl + k) % 8) // 4
        g = lax.dynamic_slice_in_dim(gain, (2 * side + core) * depth, depth, 0).astype(F32)
        t = parts.astype(F32)
        done = ((t * g).astype(BF16), jnp.sum(t * t, axis=1, keepdims=True))
        return (side, *lax.optimization_barrier(done))

    def project(side, block, square):
        weight = lax.dynamic_slice_in_dim(weights, side * columns, columns, 1)
        return jnp.dot(block, weight, preferred_element_type=F32), square

    def both_sides(near, far):
        return tuple(a + b for a, b in zip(near, far))

    def attend(low, high):
        kept = [jnp.where(first, a, b) for a, b in zip(low, high)]
        came = [swap_cores(jnp.where(first, b, a)) for a, b in zip(low, high)]
        return attention(heads, kept[0], came[0], kept[1] + came[1], tables)

    with jax.named_scope("project"):
        known = {k: project(*scaled(k, blocks[k])) for k in (0, 1, -1, 2, -2)}
        known, blocks[3], blocks[-3] = lax.optimization_barrier((known, blocks[3], blocks[-3]))
        blocks[4] = last_hop(jnp.where(first, blocks[-3], blocks[3]))
        weighted_cols = both[:, 0].reshape(64, 128)
        token_cols = both[:, 1].reshape(64, 128)
        back_w = back(weighted_cols)
        near, next_2 = known[0], both_sides(known[2], known[-2])
        next_1 = both_sides(known[1], project(*scaled(-3, blocks[-3])))
        next_3 = both_sides(known[-1], project(*scaled(3, blocks[3])))
        mixed_1, total_1 = attend(next_1, next_3)
        last_block, near, next_2, mixed_1, back_w, token_cols = lax.optimization_barrier(
            (blocks[4], near, next_2, mixed_1, back_w, token_cols)
        )
        last_block = project(*scaled(4, last_block))
        mixed_0, total_0 = attend(both_sides(near, last_block), next_2)

    with jax.named_scope("return_heads"):
        oa = send(mixed_0, lambda z, c: (z, z // 2) if c == 0 else (z + 2, z // 2))
        ob = send(mixed_1, lambda z, c: (z + 1, z // 2) if c == 0 else (z - 1, z // 2))

    with jax.named_scope("tail"):
        total = total_0 + total_1
        high = lax.reduce_precision(total, 8, 7)
        line = jnp.concatenate(
            [mixed_0[-1:], mixed_1[-1:], high.astype(BF16), (total - high).astype(BF16)], axis=0
        )
        line, ob = lax.optimization_barrier((line, ob))
        line = lax.dynamic_slice_in_dim(from_everyone(line, ("zl", "c")), 4 * core, 4, 0)
        line, oa = lax.optimization_barrier((line, oa))
        head_out = jnp.concatenate(
            [jnp.where(even, oa, ob), jnp.where(even, ob, oa)], axis=1
        )
        every = from_everyone(line, ("y", "x"))
        every = every.reshape(16, 2, 2, 4, width)
        last = every[:, :, :, :2].reshape(16, 2, 4, width)
        last = jnp.concatenate(
            [
                jnp.where(first, jnp.roll(last[:, h], h, axis=1), jnp.roll(last[:, h], h + 2, axis=1))
                for h in (0, 1)
            ],
            axis=2,
        )
        last = last.swapaxes(0, 1).reshape(64, 2 * width)
        part = jnp.dot(last, w_out, preferred_element_type=F32).astype(BF16)
        attn_last = sum_over_mp(part).astype(BF16)
        head_mean = jnp.sum(every[:, :, :, 2:].astype(F32), axis=(0, 2, 3)).reshape(-1) / TOKENS
        gap = head_mean[None] - last.astype(F32)

        def per_head(grads):
            return jnp.sum((gap * grads).reshape(64, 8, HEAD_SIZE), axis=2)

        residual = token_cols + attn_last.astype(F32)
        square = jnp.sum(residual * residual, axis=1, keepdims=True)
        product = jnp.sum(residual * weighted_cols, axis=1, keepdims=True)
        packed = jnp.concatenate(
            [
                per_head(back_w),
                per_head(back(residual)),
                jnp.broadcast_to(square, (64, 56)),
                jnp.broadcast_to(product, (64, 56)),
            ],
            axis=1,
        )
        mine = jnp.sum(lax.all_to_all(packed[:, None], DP, 0, 0, tiled=True), axis=0)
        inverse = lax.rsqrt(mine[:, 16] / MODEL_WIDTH + 1e-05)
        metric = inverse * mine[:, 72]
        scores = inverse * mine[:, :8] - (metric * inverse * inverse / MODEL_WIDTH) * mine[:, 8:16]
    return head_out, scores, metric


def solution(mesh):
    fine = Mesh(mesh.devices.reshape(4, 4, 4, 2, 2), (*DP, *MP))
    in_specs = (
        P(DP, MP),
        P(),
        P(DP, MP),
        P(DP, MP),
        P(DP, MP),
        P(MP, DP),
        P(MP),
        P(DP, MP),
        P(),
        P(),
    )
    out_specs = (P(DP, MP), P(DP, MP), P(DP))
    return jax.shard_map(
        per_device, mesh=fine, in_specs=in_specs, out_specs=out_specs, check_vma=False
    )
```

```python
import functools
import math

import jax
import jax.numpy as jnp
from jax import lax
from jax.experimental import pallas as pl
from jax.experimental.pallas import tpu as pltpu
from jax.sharding import Mesh, PartitionSpec as P

MODEL_WIDTH = 8192
HEAD_SIZE = 128
LENGTH = 256
TOKENS = 16384
DP = ("zl", "y", "x")
MP = ("zh", "c")
F32 = jnp.float32
BF16 = jnp.bfloat16


def from_everyone(value, axis):
    count = lax.axis_size(axis)
    return lax.all_to_all(
        jnp.broadcast_to(value[None], (count, *value.shape)), axis, 0, 0, tiled=True
    )


def send(value, route):
    pairs = []
    for z in range(4):
        for c in range(2):
            to = route(z, c)
            pairs.append((z * 2 + c, (to[0] % 4) * 2 + to[1]))
    return lax.ppermute(value, ("zl", "c"), pairs)


def along(value, step):
    place = lambda z: (z % 4) * 2 + z // 4
    pairs = [(place(z), place((z + step) % 8)) for z in range(8)]
    return lax.ppermute(value, ("zl", "zh"), pairs)


def to_column_owners(value, zl, m):
    got = []
    for i in range(4):
        pairs = [(a * 4 + b, b * 4 + (a + i) % 4) for a in range(4) for b in range(4)]
        got.append(lax.ppermute(value, ("zl", *MP), pairs))
    got = jnp.stack(got)
    return jnp.stack([lax.dynamic_index_in_dim(got, (m - a) % 4, 0, keepdims=False) for a in range(4)])


def sum_over_mp(value):
    others = [
        lax.ppermute(value, MP, [(i, i ^ step) for i in range(4)]).astype(F32) for step in (1, 2, 3)
    ]
    return value.astype(F32) + others[0] + (others[1] + others[2])


def swap_cores(value):
    return lax.ppermute(value, "c", [(0, 1), (1, 0)])


def rotary_tables():
    half = HEAD_SIZE // 2
    positions = jnp.arange(LENGTH, dtype=F32)
    inv_freq = jnp.exp(
        jnp.arange(half, dtype=F32) * (-2.0 * math.log(500000.0) / HEAD_SIZE)
    )
    angles = positions[:, None] * inv_freq[None, :]
    cos, sin = jnp.cos(angles), jnp.sin(angles)
    return jnp.concatenate([cos, cos], axis=1), jnp.concatenate([-sin, sin], axis=1)


def attention_kernel(heads, kept, came, squares, cos_ref, sin_ref, out, total):
    scale = lax.rsqrt(squares[...] * (1.0 / MODEL_WIDTH) + 1e-05)
    cos, sin = cos_ref[...], sin_ref[...]

    def column(i):
        at = slice(i * HEAD_SIZE, (i + 1) * HEAD_SIZE)
        return (kept[:, at] + came[:, at]) * scale

    def rotated(i):
        t = column(i)
        return (t * cos + pltpu.roll(t, HEAD_SIZE // 2, 1) * sin).astype(BF16)

    key, value = rotated(heads), column(heads + 1).astype(BF16)
    row = lax.broadcasted_iota(jnp.int32, (LENGTH, LENGTH), 0)
    causal = row >= lax.broadcasted_iota(jnp.int32, (LENGTH, LENGTH), 1)
    for h in range(heads):
        logits = lax.dot_general(
            rotated(h), key, (((1,), (1,)), ((), ())), preferred_element_type=F32
        )
        logits = jnp.where(causal, logits * (1.0 / math.sqrt(HEAD_SIZE)), -1e30)
        e = jnp.exp(logits - jnp.max(logits, axis=1, keepdims=True))
        probs = (e / jnp.sum(e, axis=1, keepdims=True)).astype(BF16)
        mixed = jnp.dot(probs, value, preferred_element_type=F32).astype(BF16)
        at = slice(h * HEAD_SIZE, (h + 1) * HEAD_SIZE)
        out[:, at] = mixed
        total[:, at] = jnp.sum(mixed.astype(F32), axis=0, keepdims=True)


def attention(heads, kept, came, squares, tables):
    return pl.pallas_call(
        functools.partial(attention_kernel, heads),
        out_shape=(
            jax.ShapeDtypeStruct((LENGTH, heads * HEAD_SIZE), BF16),
            jax.ShapeDtypeStruct((1, heads * HEAD_SIZE), F32),
        ),
        compiler_params=pltpu.CompilerParams(vmem_limit_bytes=24 * 1024 * 1024),
        cost_estimate=pl.CostEstimate(
            flops=4 * heads * LENGTH * LENGTH * HEAD_SIZE,
            bytes_accessed=2 * 4 * LENGTH * 768,
            transcendentals=heads * LENGTH * LENGTH,
        ),
    )(kept, came, squares, *tables)


def last_hop(value):
    place = lambda z, c: (z % 4) * 4 + (z // 4) * 2 + c
    pairs = [
        (place(z, c), place((z + 1 - 2 * c) % 8, c)) for z in range(8) for c in range(2)
    ]
    return lax.ppermute(value, ("zl", *MP), pairs)


def per_device(tokens, gain, w_query, w_key, w_value, w_out, final_gain, unembed, clean, corrupt):
    zh, zl, core = lax.axis_index("zh"), lax.axis_index("zl"), lax.axis_index("c")
    yx = lax.axis_index(("y", "x"))
    first = core == 0

    def back(cols):
        return lax.dot_general(
            cols.astype(BF16), w_out, (((1,), (1,)), ((), ())), preferred_element_type=F32
        )

    even = zl % 2 == 0
    width = w_query.shape[1] // 2

    with jax.named_scope("weights"):
        wkv = jnp.concatenate([w_key, w_value], axis=1)
        upper = zl // 2
        pieces = [
            jnp.concatenate(
                [lax.dynamic_slice_in_dim(w_query, h * width, width, 1), wkv], axis=1
            )
            for h in (upper, 1 - upper)
        ]
        pa = send(pieces[0], lambda z, c: (2 * c + z // 2, z % 2))
        pb = send(pieces[1], lambda z, c: (2 * c + 1 - z // 2, z % 2))
        rows = jnp.concatenate([jnp.where(even, pa, pb), jnp.where(even, pb, pa)], axis=1)
        weights = lax.all_gather(rows, ("y", "x"), axis=0, tiled=True)

    with jax.named_scope("direction"):
        vocab_rows = unembed.shape[0]
        ids = lax.axis_index(DP) * vocab_rows + jnp.arange(vocab_rows, dtype=jnp.int32)
        one_hot = (clean[:, None] == ids[None, :]).astype(F32) - (
            corrupt[:, None] == ids[None, :]
        ).astype(F32)
        found = jnp.dot(one_hot.astype(BF16), unembed, preferred_element_type=F32)
        found = found.reshape(4, 16, 16, 128).swapaxes(1, 2).astype(BF16)
        here = (jnp.arange(4) == zl)[:, None, None, None]
        own_last = jnp.where(here, tokens[LENGTH - 1].reshape(1, 16, 1, 128), 0).astype(BF16)
        packed = jnp.concatenate([found, own_last], axis=2).reshape(64, 17, 128)
        packed = lax.all_to_all(packed, DP, 0, 0, tiled=True)
        blocks = {0: tokens}
        for r in (1, 2, 3):
            for sign in (1, -1):
                blocks[-sign * r] = along(blocks[-sign * (r - 1)], sign)
            if r == 2:
                packed, *_ = lax.optimization_barrier((packed, blocks[2], blocks[-2]))
        packed = packed.astype(F32)
        packed = jnp.sum(packed.reshape(4, 16, 17, 128), axis=0)
        gain_cols = lax.dynamic_slice_in_dim(final_gain, yx * 128, 128, 0).astype(F32)
        weighted = gain_cols * jnp.sum(packed[:, :16], axis=0)
        both = jnp.stack([weighted, packed[:, 16]])
        both = to_column_owners(both, zl, 2 * zh + core)
        both, blocks[3], blocks[-3] = lax.optimization_barrier((both, blocks[3], blocks[-3]))
        blocks[4] = last_hop(jnp.where(first, blocks[-3], blocks[3]))
        weighted_cols = both[:, 0].reshape(64, 128)
        token_cols = both[:, 1].reshape(64, 128)
        back_w = back(weighted_cols)

    depth = tokens.shape[1]
    columns = width + 2 * HEAD_SIZE
    heads = width // HEAD_SIZE
    tables = rotary_tables()

    def scaled(k, parts):
        side = ((zh * 4 + zl + k) % 8) // 4
        g = lax.dynamic_slice_in_dim(gain, (2 * side + core) * depth, depth, 0).astype(F32)
        t = parts.astype(F32)
        done = ((t * g).astype(BF16), jnp.sum(t * t, axis=1, keepdims=True))
        return (side, *lax.optimization_barrier(done))

    def project(side, block, square):
        weight = lax.dynamic_slice_in_dim(weights, side * columns, columns, 1)
        return jnp.dot(block, weight, preferred_element_type=F32), square

    def both_sides(near, far):
        return tuple(a + b for a, b in zip(near, far))

    def attend(low, high):
        kept = [jnp.where(first, a, b) for a, b in zip(low, high)]
        came = [swap_cores(jnp.where(first, b, a)) for a, b in zip(low, high)]
        return attention(heads, kept[0], came[0], kept[1] + came[1], tables)

    with jax.named_scope("project"):
        known = {k: scaled(k, parts) for k, parts in blocks.items() if k != 4}
        near = project(*known[0])
        next_1, next_2, next_3 = [
            both_sides(project(*known[a]), project(*known[b])) for a, b in ((1, -3), (2, -2), (-1, 3))
        ]
        mixed_1, total_1 = attend(next_1, next_3)
        last_block, near, next_2, mixed_1, back_w, token_cols = lax.optimization_barrier(
            (blocks[4], near, next_2, mixed_1, back_w, token_cols)
        )
        last_block = project(*scaled(4, last_block))
        mixed_0, total_0 = attend(both_sides(near, last_block), next_2)

    with jax.named_scope("return_heads"):

        def owned(slot_0, slot_1):
            oa = send(slot_0, lambda z, c: (z, z // 2) if c == 0 else (z + 2, z // 2))
            ob = send(slot_1, lambda z, c: (z + 1, z // 2) if c == 0 else (z - 1, z // 2))
            return jnp.concatenate(
                [jnp.where(even, oa, ob), jnp.where(even, ob, oa)], axis=1
            )

    with jax.named_scope("tail"):
        total = total_0 + total_1
        high = lax.reduce_precision(total, 8, 7)
        line = jnp.concatenate(
            [mixed_0[-1:], mixed_1[-1:], high.astype(BF16), (total - high).astype(BF16)], axis=0
        )
        line = lax.dynamic_slice_in_dim(from_everyone(line, ("zl", "c")), 4 * core, 4, 0)
        every = from_everyone(line, ("y", "x"))
        head_out = owned(mixed_0, mixed_1)
        every, head_out = lax.optimization_barrier((every, head_out))
        every = every.reshape(16, 2, 2, 4, width)
        last = every[:, :, :, :2].reshape(16, 2, 4, width)
        last = jnp.concatenate(
            [
                jnp.where(first, jnp.roll(last[:, h], h, axis=1), jnp.roll(last[:, h], h + 2, axis=1))
                for h in (0, 1)
            ],
            axis=2,
        )
        last = last.swapaxes(0, 1).reshape(64, 2 * width)
        part = jnp.dot(last, w_out, preferred_element_type=F32).astype(BF16)
        attn_last = sum_over_mp(part).astype(BF16)
        head_mean = jnp.sum(every[:, :, :, 2:].astype(F32), axis=(0, 2, 3)).reshape(-1) / TOKENS
        gap = head_mean[None] - last.astype(F32)

        def per_head(grads):
            return jnp.sum((gap * grads).reshape(64, 8, HEAD_SIZE), axis=2)

        residual = token_cols + attn_last.astype(F32)
        square = jnp.sum(residual * residual, axis=1, keepdims=True)
        product = jnp.sum(residual * weighted_cols, axis=1, keepdims=True)
        packed = jnp.concatenate(
            [
                per_head(back_w),
                per_head(back(residual)),
                jnp.broadcast_to(square, (64, 56)),
                jnp.broadcast_to(product, (64, 56)),
            ],
            axis=1,
        )
        mine = jnp.sum(lax.all_to_all(packed[:, None], DP, 0, 0, tiled=True), axis=0)
        inverse = lax.rsqrt(mine[:, 16] / MODEL_WIDTH + 1e-05)
        metric = inverse * mine[:, 72]
        scores = inverse * mine[:, :8] - (metric * inverse * inverse / MODEL_WIDTH) * mine[:, 8:16]
    return head_out, scores, metric


def solution(mesh):
    fine = Mesh(mesh.devices.reshape(4, 4, 4, 2, 2), (*DP, *MP))
    in_specs = (
        P(DP, MP),
        P(),
        P(DP, MP),
        P(DP, MP),
        P(DP, MP),
        P(MP, DP),
        P(MP),
        P(DP, MP),
        P(),
        P(),
    )
    out_specs = (P(DP, MP), P(DP, MP), P(DP))
    return jax.shard_map(
        per_device, mesh=fine, in_specs=in_specs, out_specs=out_specs, check_vma=False
    )
```

```python
import functools
import math

import jax
import jax.numpy as jnp
from jax import lax
from jax.experimental import pallas as pl
from jax.experimental.pallas import tpu as pltpu
from jax.sharding import Mesh, PartitionSpec as P

MODEL_WIDTH = 8192
HEAD_SIZE = 128
LENGTH = 256
TOKENS = 16384
DP = ("zl", "y", "x")
MP = ("zh", "c")
F32 = jnp.float32
BF16 = jnp.bfloat16


def from_everyone(value, axis):
    count = lax.axis_size(axis)
    return lax.all_to_all(
        jnp.broadcast_to(value[None], (count, *value.shape)), axis, 0, 0, tiled=True
    )


def send(value, route):
    pairs = []
    for z in range(4):
        for c in range(2):
            to = route(z, c)
            pairs.append((z * 2 + c, (to[0] % 4) * 2 + to[1]))
    return lax.ppermute(value, ("zl", "c"), pairs)


def along(value, step):
    place = lambda z: (z % 4) * 2 + z // 4
    pairs = [(place(z), place((z + step) % 8)) for z in range(8)]
    return lax.ppermute(value, ("zl", "zh"), pairs)


def to_column_owners(value, zl, m):
    got = []
    for i in range(4):
        pairs = [(a * 4 + b, b * 4 + (a + i) % 4) for a in range(4) for b in range(4)]
        got.append(lax.ppermute(value, ("zl", *MP), pairs))
    got = jnp.stack(got)
    return jnp.stack([lax.dynamic_index_in_dim(got, (m - a) % 4, 0, keepdims=False) for a in range(4)])


def sum_over_mp(value):
    others = [
        lax.ppermute(value, MP, [(i, i ^ step) for i in range(4)]).astype(F32) for step in (1, 2, 3)
    ]
    return value.astype(F32) + others[0] + (others[1] + others[2])


def swap_cores(value):
    return lax.ppermute(value, "c", [(0, 1), (1, 0)])


def rotary_tables():
    half = HEAD_SIZE // 2
    positions = jnp.arange(LENGTH, dtype=F32)
    inv_freq = jnp.exp(
        jnp.arange(half, dtype=F32) * (-2.0 * math.log(500000.0) / HEAD_SIZE)
    )
    angles = positions[:, None] * inv_freq[None, :]
    cos, sin = jnp.cos(angles), jnp.sin(angles)
    return jnp.concatenate([cos, cos], axis=1), jnp.concatenate([-sin, sin], axis=1)


def attention_kernel(heads, kept, came, squares, cos_ref, sin_ref, out, total):
    scale = lax.rsqrt(squares[...] * (1.0 / MODEL_WIDTH) + 1e-05)
    cos, sin = cos_ref[...], sin_ref[...]

    def column(i):
        at = slice(i * HEAD_SIZE, (i + 1) * HEAD_SIZE)
        return (kept[:, at] + came[:, at]) * scale

    def rotated(i):
        t = column(i)
        return (t * cos + pltpu.roll(t, HEAD_SIZE // 2, 1) * sin).astype(BF16)

    key, value = rotated(heads), column(heads + 1).astype(BF16)
    row = lax.broadcasted_iota(jnp.int32, (LENGTH, LENGTH), 0)
    causal = row >= lax.broadcasted_iota(jnp.int32, (LENGTH, LENGTH), 1)
    for h in range(heads):
        logits = lax.dot_general(
            rotated(h), key, (((1,), (1,)), ((), ())), preferred_element_type=F32
        )
        logits = jnp.where(causal, logits * (1.0 / math.sqrt(HEAD_SIZE)), -1e30)
        e = jnp.exp(logits - jnp.max(logits, axis=1, keepdims=True))
        probs = (e / jnp.sum(e, axis=1, keepdims=True)).astype(BF16)
        mixed = jnp.dot(probs, value, preferred_element_type=F32).astype(BF16)
        at = slice(h * HEAD_SIZE, (h + 1) * HEAD_SIZE)
        out[:, at] = mixed
        total[:, at] = jnp.sum(mixed.astype(F32), axis=0, keepdims=True)


def attention(heads, kept, came, squares, tables):
    return pl.pallas_call(
        functools.partial(attention_kernel, heads),
        out_shape=(
            jax.ShapeDtypeStruct((LENGTH, heads * HEAD_SIZE), BF16),
            jax.ShapeDtypeStruct((1, heads * HEAD_SIZE), F32),
        ),
        compiler_params=pltpu.CompilerParams(vmem_limit_bytes=24 * 1024 * 1024),
        cost_estimate=pl.CostEstimate(
            flops=4 * heads * LENGTH * LENGTH * HEAD_SIZE,
            bytes_accessed=2 * 4 * LENGTH * 768,
            transcendentals=heads * LENGTH * LENGTH,
        ),
    )(kept, came, squares, *tables)


def last_hop(value):
    place = lambda z, c: (z % 4) * 4 + (z // 4) * 2 + c
    pairs = [
        (place(z, c), place((z + 1 - 2 * c) % 8, c)) for z in range(8) for c in range(2)
    ]
    return lax.ppermute(value, ("zl", *MP), pairs)


def per_device(tokens, gain, w_query, w_key, w_value, w_out, final_gain, unembed, clean, corrupt):
    zh, zl, core = lax.axis_index("zh"), lax.axis_index("zl"), lax.axis_index("c")
    yx = lax.axis_index(("y", "x"))
    first = core == 0

    def back(cols):
        return lax.dot_general(
            cols.astype(BF16), w_out, (((1,), (1,)), ((), ())), preferred_element_type=F32
        )

    even = zl % 2 == 0
    width = w_query.shape[1] // 2

    with jax.named_scope("weights"):
        wkv = jnp.concatenate([w_key, w_value], axis=1)
        upper = zl // 2
        pieces = [
            jnp.concatenate(
                [lax.dynamic_slice_in_dim(w_query, h * width, width, 1), wkv], axis=1
            )
            for h in (upper, 1 - upper)
        ]
        pa = send(pieces[0], lambda z, c: (2 * c + z // 2, z % 2))
        pb = send(pieces[1], lambda z, c: (2 * c + 1 - z // 2, z % 2))
        rows = jnp.concatenate([jnp.where(even, pa, pb), jnp.where(even, pb, pa)], axis=1)
        weights = lax.all_gather(rows, ("y", "x"), axis=0, tiled=True)

    with jax.named_scope("direction"):
        vocab_rows = unembed.shape[0]
        ids = lax.axis_index(DP) * vocab_rows + jnp.arange(vocab_rows, dtype=jnp.int32)
        one_hot = (clean[:, None] == ids[None, :]).astype(F32) - (
            corrupt[:, None] == ids[None, :]
        ).astype(F32)
        found = jnp.dot(one_hot.astype(BF16), unembed, preferred_element_type=F32)
        found = found.reshape(4, 16, 16, 128).swapaxes(1, 2).astype(BF16)
        here = (jnp.arange(4) == zl)[:, None, None, None]
        own_last = jnp.where(here, tokens[LENGTH - 1].reshape(1, 16, 1, 128), 0).astype(BF16)
        packed = jnp.concatenate([found, own_last], axis=2).reshape(64, 17, 128)
        packed = lax.all_to_all(packed, DP, 0, 0, tiled=True)
        blocks = {0: tokens}
        for r in (1, 2, 3):
            for sign in (1, -1):
                blocks[-sign * r] = along(blocks[-sign * (r - 1)], sign)
            if r == 2:
                packed, *_ = lax.optimization_barrier((packed, blocks[2], blocks[-2]))
        packed = packed.astype(F32)
        packed = jnp.sum(packed.reshape(4, 16, 17, 128), axis=0)
        gain_cols = lax.dynamic_slice_in_dim(final_gain, yx * 128, 128, 0).astype(F32)
        weighted = gain_cols * jnp.sum(packed[:, :16], axis=0)
        both = jnp.stack([weighted, packed[:, 16]])
        both = to_column_owners(both, zl, 2 * zh + core)
        both, blocks[3], blocks[-3] = lax.optimization_barrier((both, blocks[3], blocks[-3]))
        blocks[4] = last_hop(jnp.where(first, blocks[-3], blocks[3]))
        weighted_cols = both[:, 0].reshape(64, 128)
        token_cols = both[:, 1].reshape(64, 128)
        back_w = back(weighted_cols)

    depth = tokens.shape[1]
    columns = width + 2 * HEAD_SIZE
    heads = width // HEAD_SIZE
    tables = rotary_tables()

    def scaled(k, parts):
        side = ((zh * 4 + zl + k) % 8) // 4
        g = lax.dynamic_slice_in_dim(gain, (2 * side + core) * depth, depth, 0).astype(F32)
        t = parts.astype(F32)
        done = ((t * g).astype(BF16), jnp.sum(t * t, axis=1, keepdims=True))
        return (side, *lax.optimization_barrier(done))

    def project(side, block, square):
        weight = lax.dynamic_slice_in_dim(weights, side * columns, columns, 1)
        return jnp.dot(block, weight, preferred_element_type=F32), square

    def both_sides(near, far):
        return tuple(a + b for a, b in zip(near, far))

    def attend(low, high):
        kept = [jnp.where(first, a, b) for a, b in zip(low, high)]
        came = [swap_cores(jnp.where(first, b, a)) for a, b in zip(low, high)]
        return attention(heads, kept[0], came[0], kept[1] + came[1], tables)

    with jax.named_scope("project"):
        known = {k: scaled(k, parts) for k, parts in blocks.items() if k != 4}
        near = project(*known[0])
        next_1, next_2, next_3 = [
            both_sides(project(*known[a]), project(*known[b])) for a, b in ((1, -3), (2, -2), (-1, 3))
        ]
        mixed_1, total_1 = attend(next_1, next_3)
        last_block, near, next_2, mixed_1, back_w, token_cols = lax.optimization_barrier(
            (blocks[4], near, next_2, mixed_1, back_w, token_cols)
        )
        last_block = project(*scaled(4, last_block))
        mixed_0, total_0 = attend(both_sides(near, last_block), next_2)

    with jax.named_scope("return_heads"):

        def owned(slot_0, slot_1):
            oa = send(slot_0, lambda z, c: (z, z // 2) if c == 0 else (z + 2, z // 2))
            ob = send(slot_1, lambda z, c: (z + 1, z // 2) if c == 0 else (z - 1, z // 2))
            return jnp.concatenate(
                [jnp.where(even, oa, ob), jnp.where(even, ob, oa)], axis=1
            )

    with jax.named_scope("tail"):
        own = owned(
            jnp.concatenate([mixed_0[-1:], total_0.astype(BF16)], axis=0),
            jnp.concatenate([mixed_1[-1:], total_1.astype(BF16)], axis=0),
        )
        own, mixed_0 = lax.optimization_barrier((own, mixed_0))
        every = from_everyone(own, DP)
        head_out = owned(mixed_0, mixed_1)
        every, head_out = lax.optimization_barrier((every, head_out))
        last = every[:, 0]
        part = jnp.dot(last, w_out, preferred_element_type=F32).astype(BF16)
        attn_last = sum_over_mp(part).astype(BF16)
        head_mean = jnp.sum(every[:, 1].astype(F32), axis=0) / TOKENS
        gap = head_mean[None] - last.astype(F32)

        def per_head(grads):
            return jnp.sum((gap * grads).reshape(64, 8, HEAD_SIZE), axis=2)

        residual = token_cols + attn_last.astype(F32)
        square = jnp.sum(residual * residual, axis=1, keepdims=True)
        product = jnp.sum(residual * weighted_cols, axis=1, keepdims=True)
        packed = jnp.concatenate(
            [
                per_head(back_w),
                per_head(back(residual)),
                jnp.broadcast_to(square, (64, 56)),
                jnp.broadcast_to(product, (64, 56)),
            ],
            axis=1,
        )
        mine = jnp.sum(lax.all_to_all(packed[:, None], DP, 0, 0, tiled=True), axis=0)
        inverse = lax.rsqrt(mine[:, 16] / MODEL_WIDTH + 1e-05)
        metric = inverse * mine[:, 72]
        scores = inverse * mine[:, :8] - (metric * inverse * inverse / MODEL_WIDTH) * mine[:, 8:16]
    return head_out, scores, metric


def solution(mesh):
    fine = Mesh(mesh.devices.reshape(4, 4, 4, 2, 2), (*DP, *MP))
    in_specs = (
        P(DP, MP),
        P(),
        P(DP, MP),
        P(DP, MP),
        P(DP, MP),
        P(MP, DP),
        P(MP),
        P(DP, MP),
        P(),
        P(),
    )
    out_specs = (P(DP, MP), P(DP, MP), P(DP))
    return jax.shard_map(
        per_device, mesh=fine, in_specs=in_specs, out_specs=out_specs, check_vma=False
    )
```

```python
import functools
import math

import jax
import jax.numpy as jnp
from jax import lax
from jax.experimental import pallas as pl
from jax.experimental.pallas import tpu as pltpu
from jax.sharding import Mesh, PartitionSpec as P

MODEL_WIDTH = 8192
HEAD_SIZE = 128
LENGTH = 256
TOKENS = 16384
DP = ("zl", "y", "x")
MP = ("zh", "c")
F32 = jnp.float32
BF16 = jnp.bfloat16


def from_everyone(value, axis):
    count = lax.axis_size(axis)
    return lax.all_to_all(
        jnp.broadcast_to(value[None], (count, *value.shape)), axis, 0, 0, tiled=True
    )


def send(value, route):
    pairs = []
    for z in range(4):
        for c in range(2):
            to = route(z, c)
            pairs.append((z * 2 + c, (to[0] % 4) * 2 + to[1]))
    return lax.ppermute(value, ("zl", "c"), pairs)


def along(value, step):
    place = lambda z: (z % 4) * 2 + z // 4
    pairs = [(place(z), place((z + step) % 8)) for z in range(8)]
    return lax.ppermute(value, ("zl", "zh"), pairs)


def to_column_owners(value, zl, m):
    got = []
    for i in range(4):
        pairs = [(a * 4 + b, b * 4 + (a + i) % 4) for a in range(4) for b in range(4)]
        got.append(lax.ppermute(value, ("zl", *MP), pairs))
    got = jnp.stack(got)
    return jnp.stack([lax.dynamic_index_in_dim(got, (m - a) % 4, 0, keepdims=False) for a in range(4)])


def sum_over_mp(value):
    others = [
        lax.ppermute(value, MP, [(i, i ^ step) for i in range(4)]).astype(F32) for step in (1, 2, 3)
    ]
    return value.astype(F32) + others[0] + (others[1] + others[2])


def swap_cores(value):
    return lax.ppermute(value, "c", [(0, 1), (1, 0)])


def rotary_tables():
    half = HEAD_SIZE // 2
    positions = jnp.arange(LENGTH, dtype=F32)
    inv_freq = jnp.exp(
        jnp.arange(half, dtype=F32) * (-2.0 * math.log(500000.0) / HEAD_SIZE)
    )
    angles = positions[:, None] * inv_freq[None, :]
    cos, sin = jnp.cos(angles), jnp.sin(angles)
    return jnp.concatenate([cos, cos], axis=1), jnp.concatenate([-sin, sin], axis=1)


def attention_kernel(heads, kept, came, squares, cos_ref, sin_ref, out, total):
    scale = lax.rsqrt(squares[...] * (1.0 / MODEL_WIDTH) + 1e-05)
    cos, sin = cos_ref[...], sin_ref[...]

    def column(i):
        at = slice(i * HEAD_SIZE, (i + 1) * HEAD_SIZE)
        return (kept[:, at] + came[:, at]) * scale

    def rotated(i):
        t = column(i)
        return (t * cos + pltpu.roll(t, HEAD_SIZE // 2, 1) * sin).astype(BF16)

    key, value = rotated(heads), column(heads + 1).astype(BF16)
    row = lax.broadcasted_iota(jnp.int32, (LENGTH, LENGTH), 0)
    causal = row >= lax.broadcasted_iota(jnp.int32, (LENGTH, LENGTH), 1)
    for h in range(heads):
        logits = lax.dot_general(
            rotated(h), key, (((1,), (1,)), ((), ())), preferred_element_type=F32
        )
        logits = jnp.where(causal, logits * (1.0 / math.sqrt(HEAD_SIZE)), -1e30)
        e = jnp.exp(logits - jnp.max(logits, axis=1, keepdims=True))
        probs = (e / jnp.sum(e, axis=1, keepdims=True)).astype(BF16)
        mixed = jnp.dot(probs, value, preferred_element_type=F32).astype(BF16)
        at = slice(h * HEAD_SIZE, (h + 1) * HEAD_SIZE)
        out[:, at] = mixed
        total[:, at] = jnp.sum(mixed.astype(F32), axis=0, keepdims=True)


def attention(heads, kept, came, squares, tables):
    return pl.pallas_call(
        functools.partial(attention_kernel, heads),
        out_shape=(
            jax.ShapeDtypeStruct((LENGTH, heads * HEAD_SIZE), BF16),
            jax.ShapeDtypeStruct((1, heads * HEAD_SIZE), F32),
        ),
        compiler_params=pltpu.CompilerParams(vmem_limit_bytes=24 * 1024 * 1024),
        cost_estimate=pl.CostEstimate(
            flops=4 * heads * LENGTH * LENGTH * HEAD_SIZE,
            bytes_accessed=2 * 4 * LENGTH * 768,
            transcendentals=heads * LENGTH * LENGTH,
        ),
    )(kept, came, squares, *tables)


def last_hop(value):
    place = lambda z, c: (z % 4) * 4 + (z // 4) * 2 + c
    pairs = [
        (place(z, c), place((z + 1 - 2 * c) % 8, c)) for z in range(8) for c in range(2)
    ]
    return lax.ppermute(value, ("zl", *MP), pairs)


def to_line(value, zl):
    got = []
    for i in range(4):
        got.append(send(value, lambda z, c: (2 * (z % 2) + c + i, z // 2)))
    got = jnp.stack(got)
    return jnp.stack(
        [lax.dynamic_index_in_dim(got, (zl - q) % 4, 0, keepdims=False) for q in range(4)]
    )


def per_device(tokens, gain, w_query, w_key, w_value, w_out, final_gain, unembed, clean, corrupt):
    zh, zl, core = lax.axis_index("zh"), lax.axis_index("zl"), lax.axis_index("c")
    yx = lax.axis_index(("y", "x"))
    first = core == 0

    def back(cols):
        return lax.dot_general(
            cols.astype(BF16), w_out, (((1,), (1,)), ((), ())), preferred_element_type=F32
        )

    even = zl % 2 == 0
    width = w_query.shape[1] // 2

    with jax.named_scope("weights"):
        wkv = jnp.concatenate([w_key, w_value], axis=1)
        upper = zl // 2
        pieces = [
            jnp.concatenate(
                [lax.dynamic_slice_in_dim(w_query, h * width, width, 1), wkv], axis=1
            )
            for h in (upper, 1 - upper)
        ]
        pa = send(pieces[0], lambda z, c: (2 * c + z // 2, z % 2))
        pb = send(pieces[1], lambda z, c: (2 * c + 1 - z // 2, z % 2))
        rows = jnp.concatenate([jnp.where(even, pa, pb), jnp.where(even, pb, pa)], axis=1)
        weights = lax.all_gather(rows, ("y", "x"), axis=0, tiled=True)

    with jax.named_scope("direction"):
        vocab_rows = unembed.shape[0]
        ids = lax.axis_index(DP) * vocab_rows + jnp.arange(vocab_rows, dtype=jnp.int32)
        one_hot = (clean[:, None] == ids[None, :]).astype(F32) - (
            corrupt[:, None] == ids[None, :]
        ).astype(F32)
        found = jnp.dot(one_hot.astype(BF16), unembed, preferred_element_type=F32)
        found = found.reshape(4, 16, 16, 128).swapaxes(1, 2).astype(BF16)
        here = (jnp.arange(4) == zl)[:, None, None, None]
        own_last = jnp.where(here, tokens[LENGTH - 1].reshape(1, 16, 1, 128), 0).astype(BF16)
        packed = jnp.concatenate([found, own_last], axis=2).reshape(64, 17, 128)
        packed = lax.all_to_all(packed, DP, 0, 0, tiled=True)
        blocks = {0: tokens}
        for r in (1, 2, 3):
            for sign in (1, -1):
                blocks[-sign * r] = along(blocks[-sign * (r - 1)], sign)
            if r == 2:
                packed, *_ = lax.optimization_barrier((packed, blocks[2], blocks[-2]))
        packed = packed.astype(F32)
        packed = jnp.sum(packed.reshape(4, 16, 17, 128), axis=0)
        gain_cols = lax.dynamic_slice_in_dim(final_gain, yx * 128, 128, 0).astype(F32)
        weighted = gain_cols * jnp.sum(packed[:, :16], axis=0)
        both = jnp.stack([weighted, packed[:, 16]])
        both = to_column_owners(both, zl, 2 * zh + core)
        both, blocks[3], blocks[-3] = lax.optimization_barrier((both, blocks[3], blocks[-3]))
        blocks[4] = last_hop(jnp.where(first, blocks[-3], blocks[3]))
        weighted_cols = both[:, 0].reshape(64, 128)
        token_cols = both[:, 1].reshape(64, 128)
        back_w = back(weighted_cols)

    depth = tokens.shape[1]
    columns = width + 2 * HEAD_SIZE
    heads = width // HEAD_SIZE
    tables = rotary_tables()

    def scaled(k, parts):
        side = ((zh * 4 + zl + k) % 8) // 4
        g = lax.dynamic_slice_in_dim(gain, (2 * side + core) * depth, depth, 0).astype(F32)
        t = parts.astype(F32)
        done = ((t * g).astype(BF16), jnp.sum(t * t, axis=1, keepdims=True))
        return (side, *lax.optimization_barrier(done))

    def project(side, block, square):
        weight = lax.dynamic_slice_in_dim(weights, side * columns, columns, 1)
        return jnp.dot(block, weight, preferred_element_type=F32), square

    def both_sides(near, far):
        return tuple(a + b for a, b in zip(near, far))

    def attend(low, high):
        kept = [jnp.where(first, a, b) for a, b in zip(low, high)]
        came = [swap_cores(jnp.where(first, b, a)) for a, b in zip(low, high)]
        return attention(heads, kept[0], came[0], kept[1] + came[1], tables)

    with jax.named_scope("project"):
        known = {k: scaled(k, parts) for k, parts in blocks.items() if k != 4}
        near = project(*known[0])
        next_1, next_2, next_3 = [
            both_sides(project(*known[a]), project(*known[b])) for a, b in ((1, -3), (2, -2), (-1, 3))
        ]
        mixed_1, total_1 = attend(next_1, next_3)
        last_block, near, next_2, mixed_1, back_w, token_cols = lax.optimization_barrier(
            (blocks[4], near, next_2, mixed_1, back_w, token_cols)
        )
        last_block = project(*scaled(4, last_block))
        mixed_0, total_0 = attend(both_sides(near, last_block), next_2)

    with jax.named_scope("return_heads"):

        def owned(slot_0, slot_1):
            oa = send(slot_0, lambda z, c: (z, z // 2) if c == 0 else (z + 2, z // 2))
            ob = send(slot_1, lambda z, c: (z + 1, z // 2) if c == 0 else (z - 1, z // 2))
            return jnp.concatenate(
                [jnp.where(even, oa, ob), jnp.where(even, ob, oa)], axis=1
            )

    with jax.named_scope("tail"):
        total = total_0 + total_1
        high = lax.reduce_precision(total, 8, 7)
        line = jnp.concatenate(
            [mixed_0[-1:], mixed_1[-1:], high.astype(BF16), (total - high).astype(BF16)], axis=0
        )
        line, mixed_0 = lax.optimization_barrier((to_line(line, zl), mixed_0))
        every = from_everyone(line, ("y", "x"))
        head_out = owned(mixed_0, mixed_1)
        every, head_out = lax.optimization_barrier((every, head_out))
        every = every.reshape(16, 2, 2, 4, width)
        last = every[:, :, :, :2].reshape(16, 2, 4, width)
        last = jnp.concatenate(
            [
                jnp.where(first, jnp.roll(last[:, h], h, axis=1), jnp.roll(last[:, h], h + 2, axis=1))
                for h in (0, 1)
            ],
            axis=2,
        )
        last = last.swapaxes(0, 1).reshape(64, 2 * width)
        part = jnp.dot(last, w_out, preferred_element_type=F32).astype(BF16)
        attn_last = sum_over_mp(part).astype(BF16)
        head_mean = jnp.sum(every[:, :, :, 2:].astype(F32), axis=(0, 2, 3)).reshape(-1) / TOKENS
        gap = head_mean[None] - last.astype(F32)

        def per_head(grads):
            return jnp.sum((gap * grads).reshape(64, 8, HEAD_SIZE), axis=2)

        residual = token_cols + attn_last.astype(F32)
        square = jnp.sum(residual * residual, axis=1, keepdims=True)
        product = jnp.sum(residual * weighted_cols, axis=1, keepdims=True)
        packed = jnp.concatenate(
            [
                per_head(back_w),
                per_head(back(residual)),
                jnp.broadcast_to(square, (64, 56)),
                jnp.broadcast_to(product, (64, 56)),
            ],
            axis=1,
        )
        mine = jnp.sum(lax.all_to_all(packed[:, None], DP, 0, 0, tiled=True), axis=0)
        inverse = lax.rsqrt(mine[:, 16] / MODEL_WIDTH + 1e-05)
        metric = inverse * mine[:, 72]
        scores = inverse * mine[:, :8] - (metric * inverse * inverse / MODEL_WIDTH) * mine[:, 8:16]
    return head_out, scores, metric


def solution(mesh):
    fine = Mesh(mesh.devices.reshape(4, 4, 4, 2, 2), (*DP, *MP))
    in_specs = (
        P(DP, MP),
        P(),
        P(DP, MP),
        P(DP, MP),
        P(DP, MP),
        P(MP, DP),
        P(MP),
        P(DP, MP),
        P(),
        P(),
    )
    out_specs = (P(DP, MP), P(DP, MP), P(DP))
    return jax.shard_map(
        per_device, mesh=fine, in_specs=in_specs, out_specs=out_specs, check_vma=False
    )
```
